256 devices in a mesh: dp: 16 (over y, x), expert: 16 (over z, core).
Axes of the slice: x: 4, y: 4, z: 8, core: 2. Of those that a mesh axis runs over, the one named last changes fastest.
Arguments:
- tokens: bfloat16 [32768, 2048], P(('dp', 'expert')), may hold values from -6 to 6
- expert_ids: int32 [32768, 8], P(('dp', 'expert')), may hold values from 0 to 127, as said below
- gate_weights: float32 [32768, 8], P(('dp', 'expert')), may hold values from 0.1 to 1
- w_gate: bfloat16 [16, 2048, 768], P('expert'), may hold values from -0.125 to 0.125
- w_up: bfloat16 [16, 2048, 768], P('expert'), may hold values from -0.125 to 0.125
- w_down: bfloat16 [16, 768, 2048], P('expert'), may hold values from -0.21875 to 0.21875
- cotangent: bfloat16 [32768, 2048], P(('dp', 'expert')), may hold values from -6 to 6
Outputs:
- combined: bfloat16 [32768, 2048], P(('dp', 'expert'))
- grad_tokens: bfloat16 [32768, 2048], P(('dp', 'expert'))
- grad_gate: float32 [16, 2048, 768], P('expert', 'dp')
- grad_up: float32 [16, 2048, 768], P('expert', 'dp')
- grad_down: float32 [16, 768, 2048], P('expert', None, 'dp')
The draws below stay inside these ranges and needn't reach their ends.
Inputs may be any that keep to these rules, and one draw needn't show every extreme that they name: `expert_ids`: each row names 8 different experts; its k-th entry (k from 0) lies in k * 16 to (k + 1) * 16 - 1. In the rows of one device no expert is named more than 24 times. In the rows of each run of 16 devices along expert (one index of dp), one expert below 16 is named exactly 24 times by every device.
All inputs are finite; a program needn't handle non-finite values.
Results may differ from the reference program's by a relative error of at most 0.0057.
Values may be sent and summed in bfloat16 or wider, within the bound.
A program may use at most 128 MiB of HBM per device.

```python
import jax
import jax.numpy as jnp
from jax import lax

D = 2048
FF = 768
TOPK = 8
TOK_DEV = 128
GROUP = 16
CAP = 24
LIVE = 16
TOKENS = 32768
N_DP = 16
N_EXPERT = 16


def draw_expert_ids(key, part):
    key = jax.random.fold_in(key, 11)
    key_busy, key_rank, key_order, key_loose, key_rest = jax.random.split(key, 5)
    blocks = TOKENS // TOK_DEV
    busiest = jax.random.randint(key_busy, (blocks // N_EXPERT,), 0, LIVE)
    busiest = jnp.repeat(busiest, N_EXPERT)[:, None]
    positions = jnp.arange(TOK_DEV, dtype=jnp.int32)[None, :]
    scores = jax.random.randint(key_rank, (blocks, TOK_DEV), 0, 2 ** 20) * TOK_DEV + positions
    row_rank = jnp.argsort(jnp.argsort(scores, axis=1), axis=1).astype(jnp.int32)
    others = GROUP - 1
    spread = (TOK_DEV - CAP + others - 1) // others
    loose_rows = CAP - spread
    order_scores = jax.random.randint(key_order, (blocks, others), 0, 2 ** 20) * others + jnp.arange(others, dtype=jnp.int32)[None, :]
    shuffled = jnp.argsort(order_scores, axis=1).astype(jnp.int32)
    offset_rank = jnp.maximum(row_rank - CAP - loose_rows, 0)
    stratum = offset_rank * others // (TOK_DEV - CAP - loose_rows)
    fixed_value = jnp.take_along_axis(shuffled, stratum, axis=1)
    loose_value = jax.random.randint(key_loose, (blocks, TOK_DEV), 0, others)
    offset_value = jnp.where(row_rank < CAP + loose_rows, loose_value, fixed_value)
    first_column = jnp.where(row_rank < CAP, busiest, (busiest + 1 + offset_value) % GROUP)
    other_columns = GROUP * jnp.arange(1, TOPK, dtype=jnp.int32)[None, None, :] + jax.random.randint(key_rest, (blocks, TOK_DEV, TOPK - 1), 0, GROUP)
    merged = jnp.concatenate([first_column[:, :, None], other_columns], axis=2)
    return merged.reshape(TOKENS, TOPK).astype(jnp.int32)


def levels(key, dims, cuts, least, largest):
    level = 1.0
    for dim, blocks in cuts:
        heights = jax.random.uniform(jax.random.fold_in(jax.random.fold_in(key, 6), dim), (blocks,), jnp.float32, least / len(cuts), largest / len(cuts))
        level = level * jnp.repeat(jnp.exp(heights), dims[dim] // blocks).reshape((-1,) + (1,) * (len(dims) - 1 - dim))
    return level


def scatter_about(own_key, dims, scale, bound, cuts=(), held_as=jnp.bfloat16):
    drawn = jax.random.normal(own_key, dims, jnp.float32) * scale
    if len(cuts) > 0:
        drawn = levels(own_key, dims, cuts, -0.22, 0.18) * drawn
    return jnp.clip(drawn, min=-bound, max=bound).astype(held_as)


def setup_inputs(seed: int = 0) -> dict:
    key_of = jax.random.split(jax.random.key(seed), 8)
    tokens = scatter_about(key_of[0], (TOKENS, D), 1.0, 6.0, ((0, 256),))
    expert_ids = draw_expert_ids(jax.random.fold_in(key_of[7], 71), 0)
    gate_weights = jnp.clip(0.1 + 0.9 * jax.random.uniform(key_of[2], (TOKENS, TOPK), jnp.float32) ** levels(key_of[2], (TOKENS, TOPK), ((0, 256),), -0.2, 0.2), 0.1, 1.0)
    w_gate = scatter_about(key_of[3], (LIVE, D, FF), D ** -0.5, 0.125, ((0, 16),))
    w_up = scatter_about(key_of[4], (LIVE, D, FF), D ** -0.5, 0.125, ((0, 16),))
    w_down = scatter_about(key_of[5], (LIVE, FF, D), FF ** -0.5, 0.21875, ((0, 16),))
    cotangent = scatter_about(key_of[6], (TOKENS, D), 1.0, 6.0, ((0, 256),))
    return dict(tokens=tokens, expert_ids=expert_ids, gate_weights=gate_weights, w_gate=w_gate, w_up=w_up, w_down=w_down, cotangent=cotangent)


def expert_pass(tokens, cotangent, expert_ids, gate_weights, gate_w, up_w, down_w, expert_index):
    chosen = expert_ids == expert_index
    routed = jnp.any(chosen, axis=1)
    weight = jnp.sum(jnp.where(chosen, gate_weights, jnp.float32(0.0)), axis=1).astype(jnp.float32)
    positions = jnp.arange(TOKENS, dtype=jnp.int32)
    sort_key = jnp.where(routed, positions, positions + TOKENS).astype(jnp.int32)
    selected = jnp.argsort(sort_key)[: N_DP * N_EXPERT * CAP].astype(jnp.int32)
    rows_in = tokens[selected]
    row_weight = weight[selected][:, None]
    rows_grad = cotangent[selected]
    gate_pre = jnp.dot(rows_in, gate_w, preferred_element_type=jnp.float32)
    up_pre = jnp.dot(rows_in, up_w, preferred_element_type=jnp.float32)
    sigmoid_gate = jax.nn.sigmoid(gate_pre)
    activated = gate_pre * sigmoid_gate
    hidden = (activated * up_pre).astype(jnp.bfloat16)
    expert_out = jnp.dot(hidden, down_w, preferred_element_type=jnp.float32).astype(jnp.bfloat16)
    contribution = row_weight * expert_out.astype(jnp.float32)
    grad_out = (row_weight * rows_grad.astype(jnp.float32)).astype(jnp.bfloat16)
    grad_hidden = jnp.dot(grad_out, down_w.T, preferred_element_type=jnp.float32)
    grad_gate_pre = (grad_hidden * up_pre * sigmoid_gate * (1.0 + gate_pre * (1.0 - sigmoid_gate))).astype(jnp.bfloat16)
    grad_up_pre = (grad_hidden * activated).astype(jnp.bfloat16)
    grad_gate = jnp.dot(rows_in.T, grad_gate_pre, preferred_element_type=jnp.float32)
    grad_up = jnp.dot(rows_in.T, grad_up_pre, preferred_element_type=jnp.float32)
    grad_down = jnp.dot(hidden.T, grad_out, preferred_element_type=jnp.float32)
    grad_input = (jnp.dot(grad_gate_pre, gate_w.T, preferred_element_type=jnp.float32)
                  + jnp.dot(grad_up_pre, up_w.T, preferred_element_type=jnp.float32)).astype(jnp.bfloat16)
    return selected, contribution, grad_input.astype(jnp.float32), grad_gate, grad_up, grad_down


def reference(tokens, expert_ids, gate_weights, w_gate, w_up, w_down, cotangent):
    def step(carry, inputs):
        output_sum, grad_sum = carry
        expert_index, gate_w, up_w, down_w = inputs
        selected, contribution, grad_input, grad_gate, grad_up, grad_down = expert_pass(
            tokens, cotangent, expert_ids, gate_weights, gate_w, up_w, down_w, expert_index)
        output_sum = output_sum.at[selected].add(contribution)
        grad_sum = grad_sum.at[selected].add(grad_input)
        return (output_sum, grad_sum), (grad_gate, grad_up, grad_down)

    start_sums = (jnp.zeros((TOKENS, D), jnp.float32), jnp.zeros((TOKENS, D), jnp.float32))
    expert_range = jnp.arange(LIVE, dtype=jnp.int32)
    (output_sum, grad_sum), (grad_gate, grad_up, grad_down) = lax.scan(
        step, start_sums, (expert_range, w_gate, w_up, w_down))
    return output_sum.astype(jnp.bfloat16), grad_sum.astype(jnp.bfloat16), grad_gate, grad_up, grad_down
```

```python
import jax
import jax.numpy as jnp
from jax import lax
from jax.sharding import PartitionSpec as P

CAP = 24


def local(tokens, expert_ids, gate_weights, w_gate, w_up, w_down, cotangent):
    rows_here = tokens.shape[0]
    model_width = tokens.shape[1]
    groups = lax.axis_size("expert")
    per_dev = w_gate.shape[0]
    live_total = groups * per_dev
    capacity = CAP
    chosen = expert_ids[:, :1] == jnp.arange(live_total, dtype=jnp.int32)[None, :]
    hit_table = chosen.astype(jnp.float32)
    weight = gate_weights[:, :1]
    row_index = jnp.arange(rows_here, dtype=jnp.int32)
    earlier_mask = (row_index[None, :] < row_index[:, None]).astype(jnp.float32)
    before = jnp.dot(earlier_mask, hit_table, precision=lax.Precision.HIGHEST)
    slot_index = jnp.arange(capacity, dtype=jnp.float32)
    placement = hit_table.T[:, None, :] * (
        before.T[:, None, :] == slot_index[None, :, None]
    ).astype(jnp.float32)
    placement = placement.reshape(groups, per_dev, capacity, rows_here).transpose(1, 0, 2, 3)
    place_bf16 = placement.astype(jnp.bfloat16)
    outgoing = jnp.einsum(
        "enct,td->encd", place_bf16, tokens, preferred_element_type=jnp.float32
    ).astype(jnp.bfloat16)
    incoming = lax.all_to_all(outgoing, "expert", split_axis=1, concat_axis=1, tiled=True).reshape(
        per_dev, groups * capacity, model_width
    )
    gate_pre = jnp.einsum("erd,edf->erf", incoming, w_gate, preferred_element_type=jnp.float32)
    up_pre = jnp.einsum("erd,edf->erf", incoming, w_up, preferred_element_type=jnp.float32)
    sigmoid_gate = jax.nn.sigmoid(gate_pre)
    activated = gate_pre * sigmoid_gate
    hidden = (activated * up_pre).astype(jnp.bfloat16)
    result = jnp.einsum("erf,efd->erd", hidden, w_down, preferred_element_type=jnp.float32).astype(
        jnp.bfloat16
    )
    result = result.reshape(per_dev, groups, capacity, model_width)
    returned = lax.all_to_all(result, "expert", split_axis=1, concat_axis=1, tiled=True)
    combined = (weight * jnp.einsum(
        "enct,encd->td", place_bf16, returned, preferred_element_type=jnp.float32
    )).astype(jnp.bfloat16)
    grad_out = (weight * cotangent.astype(jnp.float32)).astype(jnp.bfloat16)
    scaled_grad = jnp.einsum(
        "enct,td->encd", place_bf16, grad_out, preferred_element_type=jnp.float32
    ).astype(jnp.bfloat16)
    grad_rows = lax.all_to_all(
        scaled_grad, "expert", split_axis=1, concat_axis=1, tiled=True
    ).reshape(per_dev, groups * capacity, model_width)
    grad_hidden = jnp.einsum("erd,efd->erf", grad_rows, w_down, preferred_element_type=jnp.float32)
    grad_gate_pre = (
        grad_hidden * up_pre * sigmoid_gate * (1.0 + gate_pre * (1.0 - sigmoid_gate))
    ).astype(jnp.bfloat16)
    grad_up_pre = (grad_hidden * activated).astype(jnp.bfloat16)
    grad_input = (
        jnp.einsum("erf,edf->erd", grad_gate_pre, w_gate, preferred_element_type=jnp.float32)
        + jnp.einsum("erf,edf->erd", grad_up_pre, w_up, preferred_element_type=jnp.float32)
    ).astype(jnp.bfloat16)
    grad_input = grad_input.reshape(per_dev, groups, capacity, model_width)
    local_gate = jnp.einsum(
        "erd,erf->edf", incoming, grad_gate_pre, preferred_element_type=jnp.float32
    )
    local_up = jnp.einsum("erd,erf->edf", incoming, grad_up_pre, preferred_element_type=jnp.float32)
    local_down = jnp.einsum("erf,erd->efd", hidden, grad_rows, preferred_element_type=jnp.float32)
    grad_gate, grad_up, grad_down = (
        lax.psum_scatter(part.astype(jnp.bfloat16), "dp", scatter_dimension=dim, tiled=True).astype(jnp.float32)
        for part, dim in ((local_gate, 1), (local_up, 1), (local_down, 2))
    )
    grad_back = lax.all_to_all(grad_input, "expert", split_axis=1, concat_axis=1, tiled=True)
    grad_tokens = jnp.einsum(
        "enct,encd->td", place_bf16, grad_back, preferred_element_type=jnp.float32
    ).astype(jnp.bfloat16)
    return (combined, grad_tokens, grad_gate, grad_up, grad_down)


def solution(mesh):
    in_specs = (
        P(("dp", "expert"), None),
        P(("dp", "expert"), None),
        P(("dp", "expert"), None),
        P("expert", None, None),
        P("expert", None, None),
        P("expert", None, None),
        P(("dp", "expert"), None),
    )
    out_specs = (
        P(("dp", "expert"), None),
        P(("dp", "expert"), None),
        P("expert", "dp", None),
        P("expert", "dp", None),
        P("expert", None, "dp"),
    )
    return jax.shard_map(local, mesh=mesh, in_specs=in_specs, out_specs=out_specs, check_vma=False)
```

```python
import functools

import jax
import jax.numpy as jnp
from jax import lax
from jax.experimental import pallas as pl
from jax.experimental.pallas import tpu as pltpu
from jax.sharding import PartitionSpec as P

CAP = 24
MESH = pl.DeviceIdType.MESH
F32, BF16 = jnp.float32, jnp.bfloat16
HOPS = (128, 128, 80, 32)
OFFS = (0, HOPS[0], HOPS[0] + HOPS[1], HOPS[0] + HOPS[1] + HOPS[2])
ROWS = sum(HOPS)
PAIR = 8 * CAP
TOK, COT = 0, 1
COLS = 512


def dot(a, b, ca=1, cb=0):
    return lax.dot_general(a, b, (((ca,), (cb,)), ((), ())), preferred_element_type=F32)


def kernel(
    with_dp, ids_ref, idst_ref, gw_ref, tok_ref, cot_ref, wg_hbm, wu_hbm, wd_hbm,
    comb_ref, gtok_ref, gg_ref, gu_ref, gd_ref,
    wg, wu, wd, gdn, own, ring, back, meta, sel, sel0, place, work, away, out, near, pre, hid, dgu, rs0, rs1,
    w_sem, z_send, z_recv, m_send, m_recv, p_send, p_recv, r_send, r_recv,
):
    rows, width = tok_ref.shape
    ff = hid.shape[1]
    half = ff // 2
    dp, ex = lax.axis_index("dp"), lax.axis_index("expert")
    core = lax.rem(ex, 2)
    z = lax.div(ex, 2)
    px, py = lax.rem(dp, 4), lax.div(dp, 4)

    def at_z(step):
        return (dp, lax.rem(z + step + 8, 8) * 2 + core)

    partner = (dp, z * 2 + 1 - core)

    def at_dp(axis, step):
        if axis == 0:
            return (py * 4 + lax.rem(px + step + 4, 4), ex)
        return (lax.rem(py + step + 4, 4) * 4 + px, ex)

    loads = [
        pltpu.make_async_copy(wg_hbm, wg, w_sem.at[0]),
        pltpu.make_async_copy(wu_hbm, wu, w_sem.at[1]),
        pltpu.make_async_copy(wd_hbm, wd, w_sem.at[2]),
    ]
    for load in loads:
        load.start()

    neighbours = [at_z(1), at_z(-1), partner]
    if with_dp:
        neighbours += [at_dp(0, 1), at_dp(0, -1), at_dp(1, 1), at_dp(1, -1)]
    barrier = pltpu.get_barrier_semaphore()
    for device in neighbours:
        pl.semaphore_signal(barrier, inc=1, device_id=device, device_id_type=MESH)

    def keys(e):
        odd = e & 1
        d = ((e >> 1) - z) & 7
        plus = jnp.where((d >= 1) & (d <= 3), d, jnp.where((d == 4) & (odd == 0), 4, 0))
        minus = jnp.where(d >= 5, 8 - d, jnp.where((d == 4) & (odd == 1), 4, 0))
        return odd, d, (plus, minus)

    e_c, e_r = ids_ref[:, 0:1], idst_ref[0:1, :]
    odd_c, _, key_c = keys(e_c)
    odd_r, d_r, key_r = keys(e_r)
    i0 = lax.broadcasted_iota(jnp.int32, (rows, rows), 0)
    i1 = lax.broadcasted_iota(jnp.int32, (rows, rows), 1)
    same = e_c == e_r
    rank_c = jnp.sum((same & (i1 < i0)).astype(F32), axis=1, keepdims=True)
    rank_r = jnp.sum((same & (i0 < i1)).astype(F32), axis=0, keepdims=True)
    for s in range(2):
        ahead = (key_r[s] > key_c[s]) | ((key_r[s] == key_c[s]) & (i1 < i0))
        pos = jnp.sum(ahead.astype(F32), axis=1, keepdims=True)
        hit = pos == i1.astype(F32)
        place[s] = hit.astype(BF16)
        code = jnp.where(key_c[s] > 0, (64 * key_c[s] + 24 * odd_c).astype(F32) + rank_c, 0.0)
        row = jnp.sum(jnp.where(hit, code, 0.0), axis=0, keepdims=True)
        meta[s, 0] = jnp.broadcast_to(row, meta.shape[2:])

    j = lax.broadcasted_iota(jnp.int32, (96, rows), 0)
    other = j >= 48
    j = jnp.where(other, j - 48, j)
    second = j >= CAP
    j = jnp.where(second, j - CAP, j)
    slot = (j + CAP * jnp.where(other, 1 - core, core)).astype(F32)
    slot_a = jnp.where(second, -9.0, slot)
    slot_b = jnp.where(second, slot, -9.0)
    code0 = jnp.where(d_r == 0, (24 * odd_r).astype(F32) + rank_r, -5.0)
    sel0[...] = (code0 == slot_a).astype(BF16)

    def tiles(n, body):
        def step(i, carry):
            body(i)
            return carry
        lax.fori_loop(0, n, step, 0)

    n_cols = width // COLS

    def cols(i):
        return pl.ds(pl.multiple_of(i * COLS, COLS), COLS)

    def build(kind, source):
        def body(i):
            block = source[:, cols(i)]
            for s in range(2):
                own[kind, s, :, cols(i)] = dot(place[s, :, : HOPS[0]], block, 0, 0).astype(BF16)
        tiles(n_cols, body)

    sends = []

    def send(src, dst, ssem, rsem, device, keep=True):
        copy = pltpu.make_async_remote_copy(
            src_ref=src, dst_ref=dst, send_sem=ssem, recv_sem=rsem, device_id=device, device_id_type=MESH
        )
        copy.start()
        if keep:
            sends.append(copy)
        return copy

    def part(ref, kind, s, h, n=None):
        return ref.at[kind, s, pl.ds(OFFS[h - 1], HOPS[h - 1] if n is None else n)]

    metas, moves = {}, {}

    def forward_meta(h):
        for s, step in ((0, 1), (1, -1)):
            metas[s, h] = send(
                meta.at[s, h - 1], meta.at[s, h], m_send.at[s, h - 1], m_recv.at[s, h - 1], at_z(step)
            )

    def forward(kind, h):
        for s, step in ((0, 1), (1, -1)):
            src = own.at[kind, s] if h == 1 else part(ring, kind, s, h - 1, HOPS[h - 1])
            moves[kind, s, h] = send(
                src, part(ring, kind, s, h), z_send.at[kind, s, h - 1], z_recv.at[kind, s, h - 1], at_z(step),
                keep=False,
            )

    def arrived(kind, h):
        for s in range(2):
            moves[kind, s, h].wait_recv()

    def choose(h):
        for s in range(2):
            metas[s, h].wait_recv()
        for s in range(2):
            slots = slot_b if s == 1 or h == 4 else slot_a
            sel[s, h - 1] = ((meta[s, h, 0:1, :] - 64.0 * h) == slots).astype(BF16)

    def select(kind, h):
        g = h % 4
        lo, n = OFFS[h - 1], HOPS[h - 1]
        source = (tok_ref, cot_ref)[kind]

        def body(i):
            total = dot(sel[0, h - 1, :, :n], ring[kind, 0, lo : lo + n, cols(i)]) + dot(
                sel[1, h - 1, :, :n], ring[kind, 1, lo : lo + n, cols(i)]
            )
            if h == 4:
                total = total + dot(sel0[...], source[:, cols(i)])
            total = total.astype(BF16)
            work[kind, 48 * g : 48 * g + 48, cols(i)] = total[:48]
            away[kind, 48 * g : 48 * g + 48, cols(i)] = total[48:]

        tiles(n_cols, body)

    pairs = {}

    def swap_in(kind):
        pairs[kind] = send(
            away.at[kind], work.at[kind, pl.ds(PAIR, PAIR)], p_send.at[kind], p_recv.at[kind], partner
        )

    def swap_out(kind):
        pairs[2 + kind] = send(
            out.at[kind, pl.ds(PAIR, PAIR)], near.at[kind], p_send.at[2 + kind], p_recv.at[2 + kind], partner
        )

    def group(kind, g, i):
        return jnp.concatenate(
            [out[kind, 48 * g : 48 * g + 48, cols(i)], near[kind, 48 * g : 48 * g + 48, cols(i)]], axis=0
        )

    backs = {}

    def give_back(kind, h):
        if h < 4:
            for s in range(2):
                backs[kind, s, h + 1].wait_recv()
        lo, n = OFFS[h - 1], HOPS[h - 1]

        def body(i):
            results = group(kind, h % 4, i)
            for s in range(2):
                total = dot(sel[s, h - 1, :, :n], results, 0, 0)
                if h < 4:
                    far, m = OFFS[h], HOPS[h]
                    ring[kind, s, lo : lo + m, cols(i)] = (
                        total[:m] + back[kind, s, far : far + m, cols(i)].astype(F32)
                    ).astype(BF16)
                    if m < n:
                        ring[kind, s, lo + m : lo + n, cols(i)] = total[m:].astype(BF16)
                else:
                    ring[kind, s, lo : lo + n, cols(i)] = total.astype(BF16)

        tiles(n_cols, body)
        for s, step in ((0, -1), (1, 1)):
            backs[kind, s, h] = send(
                part(ring, kind, s, h), part(back, kind, s, h),
                z_send.at[2 + kind, s, h - 1], z_recv.at[2 + kind, s, h - 1], at_z(step),
            )

    def deliver(kind, target):
        for s in range(2):
            backs[kind, s, 1].wait_recv()

        def body(i):
            total = dot(sel0[...], group(kind, 0, i), 0, 0)
            for s in range(2):
                total = total + dot(place[s, :, : HOPS[0]], back[kind, s, : HOPS[0], cols(i)])
            target[:, cols(i)] = total.astype(BF16)

        tiles(n_cols, body)

    grads = (gdn, wg, wu)
    results = (gd_ref, gg_ref, gu_ref)
    sums = {}

    def place_of(stage, side):
        axis = side if stage == 0 else 1 - side
        return axis, (px, py)[axis]

    def view(m, stage, side, dest, upper):
        c = slice(side * half, (side + 1) * half)
        if stage == 0:
            many = slice(2 * upper, 2 * upper + 2)
            return (many, dest, slice(None), c) if side == 0 else (dest, many, slice(None), c)
        many = slice(64 * upper, 64 * upper + 64)
        return (dest, px, many, c) if side == 0 else (py, dest, many, c)

    def rs_send(m, stage, side, slot):
        axis, p = place_of(stage, side)
        dest, upper, step = (
            (2, 0, 1), (1, 1, 1), (1, 0, 1), (2, 1, -1), (3, 0, -1), (3, 1, -1)
        )[slot]
        where = view(m, stage, side, lax.rem(p + dest, 4), upper)
        sums[m, stage, side, slot] = send(
            grads[m].at[where], (rs0, rs1)[stage].at[m, side, slot],
            r_send.at[m, stage, side, slot], r_recv.at[m, stage, side, slot], at_dp(axis, step),
        )

    def rs_got(m, stage, side, slot):
        sums[m, stage, side, slot].wait_recv()
        return (rs0, rs1)[stage][m, side, slot].astype(F32)

    def rs_start(m, stage):
        for slot in (0, 3, 1, 4):
            for side in range(2):
                rs_send(m, stage, side, slot)

    def rs_relay(m, stage):
        for far, dest, upper in ((0, 1, 0), (3, 3, 1)):
            for side in range(2):
                _, p = place_of(stage, side)
                where = view(m, stage, side, lax.rem(p + dest, 4), upper)
                grads[m][where] = (grads[m][where].astype(F32) + rs_got(m, stage, side, far)).astype(BF16)
                rs_send(m, stage, side, far + 2)

    def rs_finish(m, stage):
        for upper, (a, b) in enumerate(((4, 2), (1, 5))):
            for side in range(2):
                _, p = place_of(stage, side)
                where = view(m, stage, side, p, upper)
                total = grads[m][where].astype(F32) + rs_got(m, stage, side, a) + rs_got(m, stage, side, b)
                if stage == 0:
                    grads[m][where] = total.astype(BF16)
                else:
                    results[m][64 * upper : 64 * upper + 64, side * half : (side + 1) * half] = total

    build(TOK, tok_ref)
    pl.semaphore_wait(barrier, len(neighbours))
    forward_meta(1)
    forward(TOK, 1)
    build(COT, cot_ref)
    forward(COT, 1)
    for h in (1, 2, 3):
        choose(h)
        forward_meta(h + 1)
        arrived(TOK, h)
        forward(TOK, h + 1)
        arrived(COT, h)
        forward(COT, h + 1)
        select(TOK, h)
        select(COT, h)
    choose(4)
    arrived(TOK, 4)
    select(TOK, 4)
    swap_in(TOK)
    for load in loads:
        load.wait()
    pairs[TOK].wait_recv()

    def ff_tile(i):
        return pl.ds(pl.multiple_of(i * 256, 256), 256)

    def up_body(i):
        x = work[TOK]
        gate = dot(x, wg[:, :, :, ff_tile(i)].reshape(width, 256))
        up = dot(x, wu[:, :, :, ff_tile(i)].reshape(width, 256))
        pre[0, :, ff_tile(i)] = gate
        pre[1, :, ff_tile(i)] = up
        hid[:, ff_tile(i)] = (gate * jax.nn.sigmoid(gate) * up).astype(BF16)

    tiles(ff // 256, up_body)

    def down_body(i):
        out[TOK, :, cols(i)] = dot(hid[...], wd[:, cols(i)]).astype(BF16)

    tiles(n_cols, down_body)
    swap_out(TOK)

    arrived(COT, 4)
    select(COT, 4)
    swap_in(COT)
    for kind in (TOK, COT):
        for h in (1, 2, 3, 4):
            for s in range(2):
                moves[kind, s, h].wait_send()
    pairs[2 + TOK].wait_recv()
    give_back(TOK, 4)
    pairs[COT].wait_recv()

    def down_grad(i):
        gdn[i] = dot(work[COT, :, cols(i)], hid[...], 0, 0).astype(BF16).reshape(4, 128, ff)

    tiles(n_cols, down_grad)
    if with_dp:
        rs_start(0, 0)
    give_back(TOK, 3)

    def grad_body(i):
        gh = dot(work[COT], wd[ff_tile(i), :], 1, 1)
        gate, up = pre[0, :, ff_tile(i)], pre[1, :, ff_tile(i)]
        s = jax.nn.sigmoid(gate)
        dgu[:, ff_tile(i)] = (gh * up * s * (1.0 + gate * (1.0 - s))).astype(BF16)
        dgu[:, pl.ds(pl.multiple_of(ff + i * 256, 256), 256)] = (gh * (gate * s)).astype(BF16)

    tiles(ff // 256, grad_body)
    give_back(TOK, 2)

    def in_grad(i):
        total = dot(dgu[:, :ff], wg[i].reshape(COLS, ff), 1, 1) + dot(dgu[:, ff:], wu[i].reshape(COLS, ff), 1, 1)
        out[COT, :, cols(i)] = total.astype(BF16)

    tiles(n_cols, in_grad)
    swap_out(COT)
    if with_dp:
        rs_relay(0, 0)

    def up_grad(i):
        x = work[TOK, :, cols(i)]
        wg[i] = dot(x, dgu[:, :ff], 0, 0).astype(BF16).reshape(4, 128, ff)
        wu[i] = dot(x, dgu[:, ff:], 0, 0).astype(BF16).reshape(4, 128, ff)

    tiles(n_cols, up_grad)
    if with_dp:
        rs_start(1, 0)
        rs_start(2, 0)
    pairs[2 + COT].wait_recv()
    give_back(COT, 4)
    give_back(TOK, 1)
    give_back(COT, 3)
    if with_dp:
        rs_finish(0, 0)
        rs_start(0, 1)
        rs_relay(1, 0)
        rs_relay(2, 0)
        rs_relay(0, 1)
    give_back(COT, 2)
    if with_dp:
        rs_finish(1, 0)
        rs_start(1, 1)
    give_back(COT, 1)
    if with_dp:
        rs_finish(0, 1)
        rs_finish(2, 0)
        rs_start(2, 1)
        rs_relay(1, 1)
        rs_relay(2, 1)
    deliver(TOK, comb_ref)
    if with_dp:
        rs_finish(1, 1)
        rs_finish(2, 1)
    else:
        for ref in results:
            ref[...] = jnp.zeros_like(ref)
    deliver(COT, gtok_ref)
    for copy in sends:
        copy.wait_send()


def local(tokens, expert_ids, gate_weights, w_gate, w_up, w_down, cotangent):
    rows, width = tokens.shape
    ff = w_gate.shape[2]
    with_dp = lax.axis_size("dp") == 16
    shard = width // 16
    weight = gate_weights[:, :1]
    grad_out = (weight * cotangent.astype(F32)).astype(BF16)
    vmem, hbm = pl.BlockSpec(memory_space=pltpu.VMEM), pl.BlockSpec(memory_space=pl.ANY)
    dma = pltpu.SemaphoreType.DMA
    combined, grad_tokens, grad_gate, grad_up, grad_down = pl.pallas_call(
        functools.partial(kernel, with_dp),
        out_shape=(
            jax.ShapeDtypeStruct((rows, width), BF16),
            jax.ShapeDtypeStruct((rows, width), BF16),
            jax.ShapeDtypeStruct((shard, ff), F32),
            jax.ShapeDtypeStruct((shard, ff), F32),
            jax.ShapeDtypeStruct((shard, ff), F32),
        ),
        in_specs=[vmem] * 5 + [hbm] * 3,
        out_specs=(vmem,) * 5,
        scratch_shapes=[
            pltpu.VMEM((4, 4, shard, ff), BF16),
            pltpu.VMEM((4, 4, shard, ff), BF16),
            pltpu.VMEM((ff, width), BF16),
            pltpu.VMEM((4, 4, shard, ff), BF16),
            pltpu.VMEM((2, 2, HOPS[0], width), BF16),
            pltpu.VMEM((2, 2, ROWS, width), BF16),
            pltpu.VMEM((2, 2, ROWS, width), BF16),
            pltpu.VMEM((2, 5, 8, rows), F32),
            pltpu.VMEM((2, 4, 96, rows), BF16),
            pltpu.VMEM((96, rows), BF16),
            pltpu.VMEM((2, rows, rows), BF16),
            pltpu.VMEM((2, 2 * PAIR, width), BF16),
            pltpu.VMEM((2, PAIR, width), BF16),
            pltpu.VMEM((2, 2 * PAIR, width), BF16),
            pltpu.VMEM((2, PAIR, width), BF16),
            pltpu.VMEM((2, 2 * PAIR, ff), F32),
            pltpu.VMEM((2 * PAIR, ff), BF16),
            pltpu.VMEM((2 * PAIR, 2 * ff), BF16),
            pltpu.VMEM((3, 2, 6, 2, shard, ff // 2), BF16),
            pltpu.VMEM((3, 2, 6, shard // 2, ff // 2), BF16),
            dma((3,)),
            dma((4, 2, 4)),
            dma((4, 2, 4)),
            dma((2, 4)),
            dma((2, 4)),
            dma((4,)),
            dma((4,)),
            dma((3, 2, 2, 6)),
            dma((3, 2, 2, 6)),
        ],
        compiler_params=pltpu.CompilerParams(
            collective_id=0, has_side_effects=True, vmem_limit_bytes=63 * 2**20
        ),
    )(
        expert_ids, expert_ids.T, gate_weights, tokens, grad_out,
        w_gate.reshape(4, 4, shard, ff), w_up.reshape(4, 4, shard, ff), w_down.reshape(ff, width),
    )
    combined = (weight * combined.astype(F32)).astype(BF16)
    return (combined, grad_tokens, grad_gate[None], grad_up[None], grad_down.T[None])


def solution(mesh):
    in_specs = (
        P(("dp", "expert"), None),
        P(("dp", "expert"), None),
        P(("dp", "expert"), None),
        P("expert", None, None),
        P("expert", None, None),
        P("expert", None, None),
        P(("dp", "expert"), None),
    )
    out_specs = (
        P(("dp", "expert"), None),
        P(("dp", "expert"), None),
        P("expert", "dp", None),
        P("expert", "dp", None),
        P("expert", None, "dp"),
    )
    return jax.shard_map(local, mesh=mesh, in_specs=in_specs, out_specs=out_specs, check_vma=False)
```

```python
import functools

import jax
import jax.numpy as jnp
from jax import lax
from jax.experimental import pallas as pl
from jax.experimental.pallas import tpu as pltpu
from jax.sharding import PartitionSpec as P

CAP = 24
MESH = pl.DeviceIdType.MESH
F32, BF16 = jnp.float32, jnp.bfloat16
HOPS = (128, 96, 64, 32)
OFFS = (0, HOPS[0], HOPS[0] + HOPS[1], HOPS[0] + HOPS[1] + HOPS[2])
ROWS = sum(HOPS)
PAIR = 8 * CAP
TOK, COT = 0, 1
COLS = 512


def dot(a, b, ca=1, cb=0):
    return lax.dot_general(a, b, (((ca,), (cb,)), ((), ())), preferred_element_type=F32)


def kernel(
    with_dp, idst_ref, gwt_ref, tok_ref, cot_ref, wg_hbm, wu_hbm, wd_hbm,
    comb_ref, gtok_ref, gg_ref, gu_ref, gd_ref,
    wg, wu, wd, gdn, scaled, own, ring, back, meta, sel, sel0, place, work, away, out, near, pre, hid, dgu, rs0, rs1,
    w_sem, z_send, z_recv, m_send, m_recv, p_send, p_recv, r_send, r_recv,
):
    rows, width = tok_ref.shape
    ff = hid.shape[1]
    half = ff // 2
    dp, ex = lax.axis_index("dp"), lax.axis_index("expert")
    core = lax.rem(ex, 2)
    z = lax.div(ex, 2)
    px, py = lax.rem(dp, 4), lax.div(dp, 4)

    def at_z(step):
        return (dp, lax.rem(z + step + 8, 8) * 2 + core)

    partner = (dp, z * 2 + 1 - core)

    def at_dp(axis, step):
        if axis == 0:
            return (py * 4 + lax.rem(px + step + 4, 4), ex)
        return (lax.rem(py + step + 4, 4) * 4 + px, ex)

    loads = [
        pltpu.make_async_copy(wg_hbm, wg, w_sem.at[0]),
        pltpu.make_async_copy(wu_hbm, wu, w_sem.at[1]),
        pltpu.make_async_copy(wd_hbm, wd, w_sem.at[2]),
    ]
    for load in loads:
        load.start()

    neighbours = [at_z(1), at_z(-1), partner]
    if with_dp:
        neighbours += [at_dp(0, 1), at_dp(0, -1), at_dp(1, 1), at_dp(1, -1)]
    barrier = pltpu.get_barrier_semaphore()
    for device in neighbours:
        pl.semaphore_signal(barrier, inc=1, device_id=device, device_id_type=MESH)

    def distance(e):
        return ((e >> 1) - z) & 7

    i0 = lax.broadcasted_iota(jnp.int32, (rows, rows), 0)
    i1 = lax.broadcasted_iota(jnp.int32, (rows, rows), 1)

    def column(row):
        return jnp.sum(jnp.where(i0 == i1, row, jnp.zeros_like(row)), axis=1, keepdims=True)

    e_r = idst_ref[0:1, :]
    e_c = column(e_r.astype(F32)).astype(jnp.int32)
    weight = column(gwt_ref[0:1, :])
    odd_c, odd_r = e_c & 1, e_r & 1
    d_c, d_r = distance(e_c), distance(e_r)

    def count(lo, hi):
        return jnp.sum(((d_r >= lo) & (d_r <= hi)).astype(F32), axis=1, keepdims=True)

    limit = jnp.minimum(jnp.minimum(HOPS[3], HOPS[2] - count(3, 3)), HOPS[1] - count(2, 3))
    before_c = jnp.sum(((d_r == 4) & (i1 < i0)).astype(F32), axis=1, keepdims=True)
    before_r = jnp.sum(((d_c == 4) & (i0 < i1)).astype(F32), axis=0, keepdims=True)

    def keys(d, before):
        first = before < limit
        plus = jnp.where((d >= 1) & (d <= 3), d, jnp.where((d == 4) & first, 4, 0))
        minus = jnp.where(d >= 5, 8 - d, jnp.where((d == 4) & ~first, 4, 0))
        return plus, minus

    key_c, key_r = keys(d_c, before_c), keys(d_r, before_r)
    same = e_c == e_r
    rank_c = jnp.sum((same & (i1 < i0)).astype(F32), axis=1, keepdims=True)
    rank_r = jnp.sum((same & (i0 < i1)).astype(F32), axis=0, keepdims=True)
    for s in range(2):
        ahead = (key_r[s] > key_c[s]) | ((key_r[s] == key_c[s]) & (i1 < i0))
        pos = jnp.sum(ahead.astype(F32), axis=1, keepdims=True)
        hit = pos == i1.astype(F32)
        place[s] = hit.astype(BF16)
        code = jnp.where(key_c[s] > 0, (64 * key_c[s] + 24 * odd_c).astype(F32) + rank_c, 0.0)
        row = jnp.sum(jnp.where(hit, code, 0.0), axis=0, keepdims=True)
        meta[s, 0] = jnp.broadcast_to(row, meta.shape[2:])

    j = lax.broadcasted_iota(jnp.int32, (96, rows), 0)
    other = j >= 48
    j = jnp.where(other, j - 48, j)
    second = j >= CAP
    j = jnp.where(second, j - CAP, j)
    slot = (j + CAP * jnp.where(other, 1 - core, core)).astype(F32)
    slot_a = jnp.where(second, -9.0, slot)
    slot_b = jnp.where(second, slot, -9.0)
    code0 = jnp.where(d_r == 0, (24 * odd_r).astype(F32) + rank_r, -5.0)
    sel0[...] = (code0 == slot_a).astype(BF16)

    def tiles(n, body):
        def step(i, carry):
            body(i)
            return carry
        lax.fori_loop(0, n, step, 0)

    n_cols = width // COLS

    def cols(i):
        return pl.ds(pl.multiple_of(i * COLS, COLS), COLS)

    def build(kind):
        def body(i):
            if kind == TOK:
                block = tok_ref[:, cols(i)]
            else:
                block = (weight * cot_ref[:, cols(i)].astype(F32)).astype(BF16)
                scaled[:, cols(i)] = block
            for s in range(2):
                own[kind, s, :, cols(i)] = dot(place[s, :, : HOPS[0]], block, 0, 0).astype(BF16)
        tiles(n_cols, body)

    sends = []

    def send(src, dst, ssem, rsem, device, keep=True):
        copy = pltpu.make_async_remote_copy(
            src_ref=src, dst_ref=dst, send_sem=ssem, recv_sem=rsem, device_id=device, device_id_type=MESH
        )
        copy.start()
        if keep:
            sends.append(copy)
        return copy

    metas, moves = {}, {}

    def forward_meta(h):
        for s, step in ((0, 1), (1, -1)):
            metas[s, h] = send(
                meta.at[s, h - 1], meta.at[s, h], m_send.at[s, h - 1], m_recv.at[s, h - 1], at_z(step)
            )

    def chunk(q, n):
        return pl.ds(q * (width // n), width // n)

    def forward(kind, h, q=0, n=1):
        many = HOPS[h - 1]
        for s, step in ((0, 1), (1, -1)):
            src = own.at[kind, s] if h == 1 else ring.at[kind, s, pl.ds(OFFS[h - 2], many)]
            dst = ring.at[kind, s, pl.ds(OFFS[h - 1], many)]
            if n > 1:
                src, dst = src.at[:, chunk(q, n)], dst.at[:, chunk(q, n)]
            moves[kind, s, h, q] = send(
                src, dst, z_send.at[kind, s, h - 1, q], z_recv.at[kind, s, h - 1, q], at_z(step), keep=False
            )

    def arrived(kind, h, q=0):
        for s in range(2):
            moves[kind, s, h, q].wait_recv()

    def choose(h):
        for s in range(2):
            metas[s, h].wait_recv()
        for s in range(2):
            slots = slot_b if s == 1 or h == 4 else slot_a
            sel[s, h - 1] = ((meta[s, h, 0:1, :] - 64.0 * h) == slots).astype(BF16)

    def select(kind, h):
        g = h % 4
        lo, n = OFFS[h - 1], HOPS[h - 1]
        source = (tok_ref, scaled)[kind]

        def body(i):
            total = dot(sel[0, h - 1, :, :n], ring[kind, 0, lo : lo + n, cols(i)]) + dot(
                sel[1, h - 1, :, :n], ring[kind, 1, lo : lo + n, cols(i)]
            )
            if h == 4:
                total = total + dot(sel0[...], source[:, cols(i)])
            total = total.astype(BF16)
            work[kind, 48 * g : 48 * g + 48, cols(i)] = total[:48]
            away[kind, 48 * g : 48 * g + 48, cols(i)] = total[48:]

        tiles(n_cols, body)

    pairs = {}

    def swap_in(kind, g):
        pairs[kind, g] = send(
            away.at[kind, pl.ds(48 * g, 48)], work.at[kind, pl.ds(PAIR + 48 * g, 48)],
            p_send.at[kind, g], p_recv.at[kind, g], partner,
        )

    def swap_out(kind, i):
        pairs[2 + kind, i] = send(
            out.at[kind, pl.ds(PAIR, PAIR), chunk(i, 4)], near.at[kind, :, chunk(i, 4)],
            p_send.at[2 + kind, i], p_recv.at[2 + kind, i], partner,
        )

    def swapped(kind):
        for i in range(4):
            pairs[kind, i].wait_recv()

    def group(kind, g, i):
        return jnp.concatenate(
            [out[kind, 48 * g : 48 * g + 48, cols(i)], near[kind, 48 * g : 48 * g + 48, cols(i)]], axis=0
        )

    backs = {}

    def give_back(kind, h, q):
        if h < 4:
            for s in range(2):
                backs[kind, s, h + 1, q].wait_recv()
        else:
            for i in (2 * q, 2 * q + 1):
                pairs[2 + kind, i].wait_recv()
        lo, n = OFFS[h - 1], HOPS[h - 1]

        def body(k):
            i = 2 * q + k
            results = group(kind, h % 4, i)
            for s in range(2):
                total = dot(sel[s, h - 1, :, :n], results, 0, 0)
                if h < 4:
                    far, m = OFFS[h], HOPS[h]
                    ring[kind, s, lo : lo + m, cols(i)] = (
                        total[:m] + back[kind, s, far : far + m, cols(i)].astype(F32)
                    ).astype(BF16)
                    if m < n:
                        ring[kind, s, lo + m : lo + n, cols(i)] = total[m:].astype(BF16)
                else:
                    ring[kind, s, lo : lo + n, cols(i)] = total.astype(BF16)

        tiles(2, body)
        for s, step in ((0, -1), (1, 1)):
            backs[kind, s, h, q] = send(
                ring.at[kind, s, pl.ds(lo, n), chunk(q, 2)], back.at[kind, s, pl.ds(lo, n), chunk(q, 2)],
                z_send.at[2 + kind, s, h - 1, q], z_recv.at[2 + kind, s, h - 1, q], at_z(step),
            )

    def deliver(kind, target, q):
        for s in range(2):
            backs[kind, s, 1, q].wait_recv()

        def body(k):
            i = 2 * q + k
            total = dot(sel0[...], group(kind, 0, i), 0, 0)
            for s in range(2):
                total = total + dot(place[s, :, : HOPS[0]], back[kind, s, : HOPS[0], cols(i)])
            if kind == TOK:
                total = weight * total
            target[:, cols(i)] = total.astype(BF16)

        tiles(2, body)

    grads = (gdn, wg, wu)
    results = (gd_ref, gg_ref, gu_ref)
    sums = {}

    def place_of(stage, side):
        axis = side if stage == 0 else 1 - side
        return axis, (px, py)[axis]

    def view(m, stage, side, dest, upper):
        c = slice(side * half, (side + 1) * half)
        if stage == 0:
            many = slice(2 * upper, 2 * upper + 2)
            return (many, dest, slice(None), c) if side == 0 else (dest, many, slice(None), c)
        many = slice(64 * upper, 64 * upper + 64)
        return (dest, px, many, c) if side == 0 else (py, dest, many, c)

    def rs_send(m, stage, side, slot):
        axis, p = place_of(stage, side)
        dest, upper, step = (
            (2, 0, 1), (1, 1, 1), (1, 0, 1), (2, 1, -1), (3, 0, -1), (3, 1, -1)
        )[slot]
        where = view(m, stage, side, lax.rem(p + dest, 4), upper)
        sums[m, stage, side, slot] = send(
            grads[m].at[where], (rs0, rs1)[stage].at[m, side, slot],
            r_send.at[m, stage, side, slot], r_recv.at[m, stage, side, slot], at_dp(axis, step),
        )

    def rs_got(m, stage, side, slot):
        sums[m, stage, side, slot].wait_recv()
        return (rs0, rs1)[stage][m, side, slot].astype(F32)

    def rs_start(m, stage):
        for slot in (0, 3, 1, 4):
            for side in range(2):
                rs_send(m, stage, side, slot)

    def rs_relay(m, stage):
        for far, dest, upper in ((0, 1, 0), (3, 3, 1)):
            for side in range(2):
                _, p = place_of(stage, side)
                where = view(m, stage, side, lax.rem(p + dest, 4), upper)
                grads[m][where] = (grads[m][where].astype(F32) + rs_got(m, stage, side, far)).astype(BF16)
                rs_send(m, stage, side, far + 2)

    def rs_finish(m, stage):
        for side in range(2):
            _, p = place_of(stage, side)
            totals = []
            for upper, (a, b) in enumerate(((4, 2), (1, 5))):
                where = view(m, stage, side, p, upper)
                total = grads[m][where].astype(F32) + rs_got(m, stage, side, a) + rs_got(m, stage, side, b)
                if stage == 0:
                    grads[m][where] = total.astype(BF16)
                totals.append(total)
            if stage == 1:
                total = jnp.concatenate(totals, axis=0)
                c = slice(side * half, (side + 1) * half)
                if m == 0:
                    gd_ref[c, :] = total.T
                else:
                    results[m][:, c] = total

    build(TOK)
    pl.semaphore_wait(barrier, len(neighbours))
    forward_meta(1)
    forward(TOK, 1)
    build(COT)
    forward(COT, 1, 0, 4)
    for h in (1, 2, 3):
        choose(h)
        forward_meta(h + 1)
        arrived(TOK, h)
        forward(TOK, h + 1)
        forward(COT, 1, h, 4)
        select(TOK, h)
        swap_in(TOK, h)
    choose(4)
    arrived(TOK, 4)
    select(TOK, 4)
    swap_in(TOK, 0)
    for load in loads:
        load.wait()
    swapped(TOK)
    for q in range(4):
        arrived(COT, 1, q)
        if q % 2:
            forward(COT, 2, q // 2, 2)

    def ff_tile(i):
        return pl.ds(pl.multiple_of(i * 256, 256), 256)

    def up_body(i):
        x = work[TOK]
        gate = dot(x, wg[:, :, :, ff_tile(i)].reshape(width, 256))
        up = dot(x, wu[:, :, :, ff_tile(i)].reshape(width, 256))
        pre[0, :, ff_tile(i)] = gate
        pre[1, :, ff_tile(i)] = up
        hid[:, ff_tile(i)] = (gate * jax.nn.sigmoid(gate) * up).astype(BF16)

    tiles(ff // 256, up_body)
    for i in range(n_cols):
        c = slice(i * COLS, (i + 1) * COLS)
        out[TOK, :, c] = dot(hid[...], wd[:, c]).astype(BF16)
        swap_out(TOK, i)
    select(COT, 1)
    swap_in(COT, 1)
    arrived(COT, 2, 0)
    forward(COT, 3, 0, 2)

    for s in range(2):
        for h in (1, 2, 3, 4):
            moves[TOK, s, h, 0].wait_send()
    give_back(TOK, 4, 0)
    arrived(COT, 2, 1)
    forward(COT, 3, 1, 2)
    give_back(TOK, 4, 1)
    select(COT, 2)
    swap_in(COT, 2)
    arrived(COT, 3, 0)
    forward(COT, 4, 0, 2)
    arrived(COT, 3, 1)
    forward(COT, 4, 1, 2)
    give_back(TOK, 3, 0)
    give_back(TOK, 3, 1)
    select(COT, 3)
    swap_in(COT, 3)
    arrived(COT, 4, 0)
    arrived(COT, 4, 1)
    select(COT, 4)
    swap_in(COT, 0)
    for s in range(2):
        for h, q in ((1, 0), (1, 1), (1, 2), (1, 3), (2, 0), (2, 1), (3, 0), (3, 1), (4, 0), (4, 1)):
            moves[COT, s, h, q].wait_send()
    swapped(COT)

    def down_grad(i):
        gdn[i] = dot(work[COT, :, cols(i)], hid[...], 0, 0).astype(BF16).reshape(4, 128, ff)

    tiles(n_cols, down_grad)
    if with_dp:
        rs_start(0, 0)
    give_back(TOK, 2, 0)
    give_back(TOK, 2, 1)

    def grad_body(i):
        gh = dot(work[COT], wd[ff_tile(i), :], 1, 1)
        gate, up = pre[0, :, ff_tile(i)], pre[1, :, ff_tile(i)]
        s = jax.nn.sigmoid(gate)
        dgu[:, ff_tile(i)] = (gh * up * s * (1.0 + gate * (1.0 - s))).astype(BF16)
        dgu[:, pl.ds(pl.multiple_of(ff + i * 256, 256), 256)] = (gh * (gate * s)).astype(BF16)

    tiles(ff // 256, grad_body)
    for i in range(n_cols):
        total = dot(dgu[:, :ff], wg[i].reshape(COLS, ff), 1, 1) + dot(dgu[:, ff:], wu[i].reshape(COLS, ff), 1, 1)
        out[COT, :, i * COLS : (i + 1) * COLS] = total.astype(BF16)
        swap_out(COT, i)
    if with_dp:
        rs_relay(0, 0)

    def up_grad(i):
        x = work[TOK, :, cols(i)]
        wg[i] = dot(x, dgu[:, :ff], 0, 0).astype(BF16).reshape(4, 128, ff)
        wu[i] = dot(x, dgu[:, ff:], 0, 0).astype(BF16).reshape(4, 128, ff)

    tiles(n_cols, up_grad)
    if with_dp:
        rs_start(1, 0)
    give_back(COT, 4, 0)
    give_back(COT, 4, 1)
    give_back(TOK, 1, 0)
    give_back(TOK, 1, 1)
    if with_dp:
        rs_finish(0, 0)
        rs_start(0, 1)
        rs_relay(1, 0)
        rs_start(2, 0)
    give_back(COT, 3, 0)
    give_back(COT, 3, 1)
    if with_dp:
        rs_relay(0, 1)
        rs_finish(1, 0)
        rs_start(1, 1)
        rs_relay(2, 0)
    give_back(COT, 2, 0)
    give_back(COT, 2, 1)
    if with_dp:
        rs_finish(0, 1)
        rs_relay(1, 1)
    deliver(TOK, comb_ref, 0)
    deliver(TOK, comb_ref, 1)
    give_back(COT, 1, 0)
    give_back(COT, 1, 1)
    if with_dp:
        rs_finish(2, 0)
        rs_start(2, 1)
        rs_finish(1, 1)
        rs_relay(2, 1)
        rs_finish(2, 1)
    else:
        for ref in results:
            ref[...] = jnp.zeros_like(ref)
    deliver(COT, gtok_ref, 0)
    deliver(COT, gtok_ref, 1)
    for copy in sends:
        copy.wait_send()


def hand_over(*refs):
    n = (len(refs) - 1) // 3
    sources, targets, held, sems = refs[:n], refs[n : 2 * n], refs[2 * n : 3 * n], refs[-1]

    def copies(a, b, step):
        every = []
        for i in range(n):
            many = a[i].shape[0] // 2
            for k in range(2):
                piece = pl.ds(k * many, many)
                every.append(pltpu.make_async_copy(a[i].at[piece], b[i].at[piece], sems.at[step, i, k]))
        return every

    loads, stores = copies(sources, held, 0), copies(held, targets, 1)
    for load in loads:
        load.start()
    for load, store in zip(loads, stores):
        load.wait()
        store.start()
    for store in stores:
        store.wait()


def local(tokens, expert_ids, gate_weights, w_gate, w_up, w_down, cotangent):
    rows, width = tokens.shape
    ff = w_gate.shape[2]
    with_dp = lax.axis_size("dp") == 16
    shard = width // 16
    vmem, hbm = pl.BlockSpec(memory_space=pltpu.VMEM), pl.BlockSpec(memory_space=pl.ANY)
    dma = pltpu.SemaphoreType.DMA
    shapes = (
        jax.ShapeDtypeStruct((rows, width), BF16),
        jax.ShapeDtypeStruct((rows, width), BF16),
        jax.ShapeDtypeStruct((shard, ff), F32),
        jax.ShapeDtypeStruct((shard, ff), F32),
        jax.ShapeDtypeStruct((ff, shard), F32),
    )
    outs = pl.pallas_call(
        functools.partial(kernel, with_dp),
        out_shape=shapes,
        in_specs=[vmem] * 4 + [hbm] * 3,
        out_specs=(vmem,) * 5,
        scratch_shapes=[
            pltpu.VMEM((4, 4, shard, ff), BF16),
            pltpu.VMEM((4, 4, shard, ff), BF16),
            pltpu.VMEM((ff, width), BF16),
            pltpu.VMEM((4, 4, shard, ff), BF16),
            pltpu.VMEM((rows, width), BF16),
            pltpu.VMEM((2, 2, HOPS[0], width), BF16),
            pltpu.VMEM((2, 2, ROWS, width), BF16),
            pltpu.VMEM((2, 2, ROWS, width), BF16),
            pltpu.VMEM((2, 5, 8, rows), F32),
            pltpu.VMEM((2, 4, 96, rows), BF16),
            pltpu.VMEM((96, rows), BF16),
            pltpu.VMEM((2, rows, rows), BF16),
            pltpu.VMEM((2, 2 * PAIR, width), BF16),
            pltpu.VMEM((2, PAIR, width), BF16),
            pltpu.VMEM((2, 2 * PAIR, width), BF16),
            pltpu.VMEM((2, PAIR, width), BF16),
            pltpu.VMEM((2, 2 * PAIR, ff), F32),
            pltpu.VMEM((2 * PAIR, ff), BF16),
            pltpu.VMEM((2 * PAIR, 2 * ff), BF16),
            pltpu.VMEM((3, 2, 6, 2, shard, ff // 2), BF16),
            pltpu.VMEM((3, 2, 6, shard // 2, ff // 2), BF16),
            dma((3,)),
            dma((4, 2, 4, 4)),
            dma((4, 2, 4, 4)),
            dma((2, 4)),
            dma((2, 4)),
            dma((4, 4)),
            dma((4, 4)),
            dma((3, 2, 2, 6)),
            dma((3, 2, 2, 6)),
        ],
        compiler_params=pltpu.CompilerParams(
            collective_id=0, has_side_effects=True, vmem_limit_bytes=63 * 2**20
        ),
    )(
        expert_ids.T, gate_weights.T, tokens, cotangent,
        w_gate.reshape(4, 4, shard, ff), w_up.reshape(4, 4, shard, ff), w_down.reshape(ff, width),
    )
    combined, grad_tokens, grad_gate, grad_up, grad_down = pl.pallas_call(
        hand_over,
        out_shape=shapes,
        in_specs=[hbm] * 5,
        out_specs=(hbm,) * 5,
        scratch_shapes=[pltpu.VMEM(s.shape, s.dtype) for s in shapes] + [dma((2, 5, 2))],
    )(*outs)
    return (combined, grad_tokens, grad_gate[None], grad_up[None], grad_down[None])


def solution(mesh):
    in_specs = (
        P(("dp", "expert"), None),
        P(("dp", "expert"), None),
        P(("dp", "expert"), None),
        P("expert", None, None),
        P("expert", None, None),
        P("expert", None, None),
        P(("dp", "expert"), None),
    )
    out_specs = (
        P(("dp", "expert"), None),
        P(("dp", "expert"), None),
        P("expert", "dp", None),
        P("expert", "dp", None),
        P("expert", None, "dp"),
    )
    return jax.shard_map(local, mesh=mesh, in_specs=in_specs, out_specs=out_specs, check_vma=False)
```

```python
import functools

import jax
import jax.numpy as jnp
from jax import lax
from jax.experimental import pallas as pl
from jax.experimental.pallas import tpu as pltpu
from jax.sharding import PartitionSpec as P

CAP = 24
MESH = pl.DeviceIdType.MESH
F32, BF16 = jnp.float32, jnp.bfloat16
HOPS = (128, 96, 64, 32)
OFFS = (0, HOPS[0], HOPS[0] + HOPS[1], HOPS[0] + HOPS[1] + HOPS[2])
ROWS = sum(HOPS)
PAIR = 8 * CAP
TOK, COT = 0, 1
COLS = 512


def dot(a, b, ca=1, cb=0):
    return lax.dot_general(a, b, (((ca,), (cb,)), ((), ())), preferred_element_type=F32)


def kernel(
    with_dp, idst_ref, gwt_ref, tok_ref, cot_ref, wg_hbm, wu_hbm, wd_hbm,
    comb_hbm, gtok_hbm, gg_hbm, gu_hbm, gd_hbm, comb_ref, gtok_ref, gg_ref, gu_ref, gd_ref,
    wg, wu, wd, gdn, ggt, gup, scaled, own, ring, back, meta, sel, sel0, place, work, away, out, near, pre, hid, dgu, x_t, hid_t, rs0, rs1, rs0d, rs1d,
    w_sem, o_sem, z_send, z_recv, m_send, m_recv, p_send, p_recv, r_send, r_recv,
):
    rows, width = tok_ref.shape
    ff = hid.shape[1]
    half = ff // 2
    dp, ex = lax.axis_index("dp"), lax.axis_index("expert")
    core = lax.rem(ex, 2)
    z = lax.div(ex, 2)
    px, py = lax.rem(dp, 4), lax.div(dp, 4)

    def at_z(step):
        return (dp, lax.rem(z + step + 8, 8) * 2 + core)

    partner = (dp, z * 2 + 1 - core)

    def at_dp(axis, step):
        if axis == 0:
            return (py * 4 + lax.rem(px + step + 4, 4), ex)
        return (lax.rem(py + step + 4, 4) * 4 + px, ex)

    loads = [
        pltpu.make_async_copy(wg_hbm, wg, w_sem.at[0]),
        pltpu.make_async_copy(wu_hbm, wu, w_sem.at[1]),
        pltpu.make_async_copy(wd_hbm, wd, w_sem.at[2]),
    ]
    for load in loads:
        load.start()

    neighbours = [at_z(1), at_z(-1), partner]
    if with_dp:
        neighbours += [at_dp(0, 1), at_dp(0, -1), at_dp(1, 1), at_dp(1, -1)]
    barrier = pltpu.get_barrier_semaphore()
    for device in neighbours:
        pl.semaphore_signal(barrier, inc=1, device_id=device, device_id_type=MESH)

    def distance(e):
        return ((e >> 1) - z) & 7

    i0 = lax.broadcasted_iota(jnp.int32, (rows, rows), 0)
    i1 = lax.broadcasted_iota(jnp.int32, (rows, rows), 1)

    def column(row):
        return jnp.sum(jnp.where(i0 == i1, row, jnp.zeros_like(row)), axis=1, keepdims=True)

    e_r = idst_ref[0:1, :]
    e_c = column(e_r.astype(F32)).astype(jnp.int32)
    weight = column(gwt_ref[0:1, :])
    odd_c, odd_r = e_c & 1, e_r & 1
    d_c, d_r = distance(e_c), distance(e_r)

    def count(lo, hi):
        return jnp.sum(((d_r >= lo) & (d_r <= hi)).astype(F32), axis=1, keepdims=True)

    limit = jnp.minimum(jnp.minimum(HOPS[3], HOPS[2] - count(3, 3)), HOPS[1] - count(2, 3))
    before_c = jnp.sum(((d_r == 4) & (i1 < i0)).astype(F32), axis=1, keepdims=True)
    before_r = jnp.sum(((d_c == 4) & (i0 < i1)).astype(F32), axis=0, keepdims=True)

    def keys(d, before):
        first = before < limit
        plus = jnp.where((d >= 1) & (d <= 3), d, jnp.where((d == 4) & first, 4, 0))
        minus = jnp.where(d >= 5, 8 - d, jnp.where((d == 4) & ~first, 4, 0))
        return plus, minus

    key_c, key_r = keys(d_c, before_c), keys(d_r, before_r)
    same = e_c == e_r
    rank_c = jnp.sum((same & (i1 < i0)).astype(F32), axis=1, keepdims=True)
    rank_r = jnp.sum((same & (i0 < i1)).astype(F32), axis=0, keepdims=True)
    for s in range(2):
        ahead = (key_r[s] > key_c[s]) | ((key_r[s] == key_c[s]) & (i1 < i0))
        pos = jnp.sum(ahead.astype(F32), axis=1, keepdims=True)
        hit = pos == i1.astype(F32)
        place[s] = hit.astype(BF16)
        code = jnp.where(key_c[s] > 0, (64 * key_c[s] + 24 * odd_c).astype(F32) + rank_c, 0.0)
        row = jnp.sum(jnp.where(hit, code, 0.0), axis=0, keepdims=True)
        meta[s, 0] = jnp.broadcast_to(row, meta.shape[2:])

    j = lax.broadcasted_iota(jnp.int32, (96, rows), 0)
    other = j >= 48
    j = jnp.where(other, j - 48, j)
    second = j >= CAP
    j = jnp.where(second, j - CAP, j)
    slot = (j + CAP * jnp.where(other, 1 - core, core)).astype(F32)
    slot_a = jnp.where(second, -9.0, slot)
    slot_b = jnp.where(second, slot, -9.0)
    code0 = jnp.where(d_r == 0, (24 * odd_r).astype(F32) + rank_r, -5.0)
    sel0[...] = (code0 == slot_a).astype(BF16)

    def tiles(n, body):
        def step(i, carry):
            body(i)
            return carry
        lax.fori_loop(0, n, step, 0)

    n_cols = width // COLS

    def cols(i):
        return pl.ds(pl.multiple_of(i * COLS, COLS), COLS)

    def build(kind, i):
        c = slice(i * COLS, (i + 1) * COLS)
        if kind == TOK:
            block = tok_ref[:, c]
        else:
            block = (weight * cot_ref[:, c].astype(F32)).astype(BF16)
            scaled[:, c] = block
        for s in range(2):
            own[kind, s, :, c] = dot(place[s], block, 0, 0).astype(BF16)

    sends = []

    def send(src, dst, ssem, rsem, device, keep=True):
        copy = pltpu.make_async_remote_copy(
            src_ref=src, dst_ref=dst, send_sem=ssem, recv_sem=rsem, device_id=device, device_id_type=MESH
        )
        copy.start()
        if keep:
            sends.append(copy)
        return copy

    metas, moves = {}, {}

    def forward_meta(h):
        for s, step in ((0, 1), (1, -1)):
            metas[s, h] = send(
                meta.at[s, h - 1], meta.at[s, h], m_send.at[s, h - 1], m_recv.at[s, h - 1], at_z(step)
            )

    stores = []

    def store(src, dst):
        copy = pltpu.make_async_copy(src, dst, o_sem.at[len(stores)])
        copy.start()
        stores.append(copy)

    def chunk(q, n):
        return pl.ds(q * (width // n), width // n)

    def forward(kind, h, q=0, n=1):
        many = HOPS[h - 1]
        for s, step in ((0, 1), (1, -1)):
            src = own.at[kind, s] if h == 1 else ring.at[kind, s, pl.ds(OFFS[h - 2], many)]
            dst = ring.at[kind, s, pl.ds(OFFS[h - 1], many)]
            if n > 1:
                src, dst = src.at[:, chunk(q, n)], dst.at[:, chunk(q, n)]
            moves[kind, s, h, q] = send(
                src, dst, z_send.at[kind, s, h - 1, q], z_recv.at[kind, s, h - 1, q], at_z(step), keep=False
            )

    def arrived(kind, h, q=0):
        for s in range(2):
            moves[kind, s, h, q].wait_recv()

    def choose(h):
        for s in range(2):
            metas[s, h].wait_recv()
        for s in range(2):
            slots = slot_b if s == 1 or h == 4 else slot_a
            sel[s, h - 1] = ((meta[s, h, 0:1, :] - 64.0 * h) == slots).astype(BF16)

    def select(kind, h):
        g = h % 4
        lo, n = OFFS[h - 1], HOPS[h - 1]
        source = (tok_ref, scaled)[kind]

        def body(i):
            total = dot(sel[0, h - 1, :, :n], ring[kind, 0, lo : lo + n, cols(i)]) + dot(
                sel[1, h - 1, :, :n], ring[kind, 1, lo : lo + n, cols(i)]
            )
            if h == 4:
                total = total + dot(sel0[...], source[:, cols(i)])
            total = total.astype(BF16)
            work[kind, 48 * g : 48 * g + 48, cols(i)] = total[:48]
            away[kind, 48 * g : 48 * g + 48, cols(i)] = total[48:]

        tiles(n_cols, body)

    pairs = {}

    def swap_in(kind, g):
        pairs[kind, g] = send(
            away.at[kind, pl.ds(48 * g, 48)], work.at[kind, pl.ds(PAIR + 48 * g, 48)],
            p_send.at[kind, g], p_recv.at[kind, g], partner,
        )

    def swap_out(kind, i):
        pairs[2 + kind, i] = send(
            out.at[kind, pl.ds(PAIR, PAIR), chunk(i, 4)], near.at[kind, :, chunk(i, 4)],
            p_send.at[2 + kind, i], p_recv.at[2 + kind, i], partner,
        )

    def swapped(kind):
        for i in range(4):
            pairs[kind, i].wait_recv()

    def group(kind, g, i):
        return jnp.concatenate(
            [out[kind, 48 * g : 48 * g + 48, cols(i)], near[kind, 48 * g : 48 * g + 48, cols(i)]], axis=0
        )

    backs = {}

    def give_back(kind, h, q):
        if h < 4:
            for s in range(2):
                backs[kind, s, h + 1, q].wait_recv()
        else:
            for i in (2 * q, 2 * q + 1):
                pairs[2 + kind, i].wait_recv()
        lo, n = OFFS[h - 1], HOPS[h - 1]

        def body(k):
            i = 2 * q + k
            results = group(kind, h % 4, i)
            for s in range(2):
                total = dot(sel[s, h - 1, :, :n], results, 0, 0)
                if h < 4:
                    far, m = OFFS[h], HOPS[h]
                    ring[kind, s, lo : lo + m, cols(i)] = (
                        total[:m] + back[kind, s, far : far + m, cols(i)].astype(F32)
                    ).astype(BF16)
                    if m < n:
                        ring[kind, s, lo + m : lo + n, cols(i)] = total[m:].astype(BF16)
                else:
                    ring[kind, s, lo : lo + n, cols(i)] = total.astype(BF16)

        tiles(2, body)
        for s, step in ((0, -1), (1, 1)):
            backs[kind, s, h, q] = send(
                ring.at[kind, s, pl.ds(lo, n), chunk(q, 2)], back.at[kind, s, pl.ds(lo, n), chunk(q, 2)],
                z_send.at[2 + kind, s, h - 1, q], z_recv.at[2 + kind, s, h - 1, q], at_z(step),
            )

    def deliver(kind, target, q):
        for s in range(2):
            backs[kind, s, 1, q].wait_recv()

        def body(k):
            i = 2 * q + k
            total = dot(sel0[...], group(kind, 0, i), 0, 0)
            for s in range(2):
                total = total + dot(place[s, :, : HOPS[0]], back[kind, s, : HOPS[0], cols(i)])
            if kind == TOK:
                total = weight * total
            target[:, cols(i)] = total.astype(BF16)

        tiles(2, body)
        store(target.at[:, chunk(q, 2)], (comb_hbm, gtok_hbm)[kind].at[:, chunk(q, 2)])

    grads = (gdn, ggt, gup)
    results = (gd_ref, gg_ref, gu_ref)
    sums = {}

    def place_of(stage, side):
        axis = side if stage == 0 else 1 - side
        return axis, (px, py)[axis]

    def view(m, stage, side, dest, upper):
        c = slice(side * half, (side + 1) * half)
        if m == 0:
            if stage == 0:
                many = slice(2 * upper, 2 * upper + 2)
                return (many, dest, c) if side == 0 else (dest, many, c)
            part = slice(side * half + upper * (half // 2), side * half + (upper + 1) * (half // 2))
            return (dest, px, part) if side == 0 else (py, dest, part)
        if stage == 0:
            many = slice(2 * upper, 2 * upper + 2)
            return (many, dest, slice(None), c) if side == 0 else (dest, many, slice(None), c)
        many = slice(64 * upper, 64 * upper + 64)
        return (dest, px, many, c) if side == 0 else (py, dest, many, c)

    def inbox(m, stage):
        return ((rs0d, rs1d) if m == 0 else (rs0.at[m - 1], rs1.at[m - 1]))[stage]

    def rs_send(m, stage, side, slot):
        axis, p = place_of(stage, side)
        dest, upper, step = (
            (2, 0, 1), (1, 1, 1), (1, 0, 1), (2, 1, -1), (3, 0, -1), (3, 1, -1)
        )[slot]
        where = view(m, stage, side, lax.rem(p + dest, 4), upper)
        sums[m, stage, side, slot] = send(
            grads[m].at[where], inbox(m, stage).at[side, slot],
            r_send.at[m, stage, side, slot], r_recv.at[m, stage, side, slot], at_dp(axis, step),
        )

    def rs_got(m, stage, side, slot):
        sums[m, stage, side, slot].wait_recv()
        return inbox(m, stage)[side, slot].astype(F32)

    def rs_start(m, stage, slots=(0, 3, 1, 4)):
        for slot in slots:
            for side in range(2):
                rs_send(m, stage, side, slot)

    def rs_relay(m, stage):
        for far, dest, upper in ((0, 1, 0), (3, 3, 1)):
            for side in range(2):
                _, p = place_of(stage, side)
                where = view(m, stage, side, lax.rem(p + dest, 4), upper)
                grads[m][where] = (grads[m][where].astype(F32) + rs_got(m, stage, side, far)).astype(BF16)
                rs_send(m, stage, side, far + 2)

    def rs_finish(m, stage):
        for side in range(2):
            _, p = place_of(stage, side)
            totals = []
            for upper, (a, b) in enumerate(((4, 2), (1, 5))):
                where = view(m, stage, side, p, upper)
                total = grads[m][where].astype(F32) + rs_got(m, stage, side, a) + rs_got(m, stage, side, b)
                if stage == 0:
                    grads[m][where] = total.astype(BF16)
                totals.append(total)
            if stage == 1:
                total = jnp.concatenate(totals, axis=0)
                c = slice(side * half, (side + 1) * half)
                if m == 0:
                    gd_ref[c, :] = total
                else:
                    results[m][:, c] = total
        if stage == 1:
            store(results[m], (gd_hbm, gg_hbm, gu_hbm)[m])

    build(TOK, 0)
    pl.semaphore_wait(barrier, len(neighbours))
    forward_meta(1)
    forward(TOK, 1, 0, 4)
    for i in range(1, 4):
        build(TOK, i)
        forward(TOK, 1, i, 4)
    for i in range(4):
        build(COT, i)
    forward(COT, 1, 0, 4)
    for h in (1, 2, 3):
        choose(h)
        forward_meta(h + 1)
        for q in range(4 if h == 1 else 1):
            arrived(TOK, h, q)
        forward(TOK, h + 1)
        forward(COT, 1, h, 4)
        if h == 3:
            arrived(COT, 1, 0)
            arrived(COT, 1, 1)
            forward(COT, 2, 0, 2)
        select(TOK, h)
        swap_in(TOK, h)
    choose(4)
    arrived(TOK, 4)
    select(TOK, 4)
    swap_in(TOK, 0)
    for load in loads:
        load.wait()
    arrived(COT, 1, 2)
    arrived(COT, 1, 3)
    forward(COT, 2, 1, 2)
    swapped(TOK)

    def ff_tile(i):
        return pl.ds(pl.multiple_of(i * 256, 256), 256)

    def up_body(i):
        x = work[TOK]
        gate = dot(x, wg[:, :, :, ff_tile(i)].reshape(width, 256))
        up = dot(x, wu[:, :, :, ff_tile(i)].reshape(width, 256))
        pre[0, :, ff_tile(i)] = gate
        pre[1, :, ff_tile(i)] = up
        hid[:, ff_tile(i)] = (gate * jax.nn.sigmoid(gate) * up).astype(BF16)

    tiles(ff // 256, up_body)
    for i in range(n_cols):
        c = slice(i * COLS, (i + 1) * COLS)
        out[TOK, :, c] = dot(hid[...], wd[:, c]).astype(BF16)
        swap_out(TOK, i)
    arrived(COT, 2, 0)
    forward(COT, 3, 0, 2)
    select(COT, 1)
    swap_in(COT, 1)
    arrived(COT, 2, 1)
    forward(COT, 3, 1, 2)

    for s in range(2):
        for h, q in ((1, 0), (1, 1), (1, 2), (1, 3), (2, 0), (3, 0), (4, 0)):
            moves[TOK, s, h, q].wait_send()
    give_back(TOK, 4, 0)
    hid_t[...] = hid[...].T

    def turn(i):
        x_t[cols(i), :] = work[TOK, :, cols(i)].T

    arrived(COT, 3, 0)
    forward(COT, 4, 0, 2)
    select(COT, 2)
    swap_in(COT, 2)
    arrived(COT, 3, 1)
    forward(COT, 4, 1, 2)
    give_back(TOK, 4, 1)
    tiles(n_cols, turn)
    select(COT, 3)
    swap_in(COT, 3)
    give_back(TOK, 3, 0)
    arrived(COT, 4, 0)
    arrived(COT, 4, 1)
    select(COT, 4)
    swap_in(COT, 0)
    for s in range(2):
        for h, q in ((1, 0), (1, 1), (1, 2), (1, 3), (2, 0), (2, 1), (3, 0), (3, 1), (4, 0), (4, 1)):
            moves[COT, s, h, q].wait_send()
    give_back(TOK, 3, 1)
    swapped(COT)

    def down_grad(i):
        total = dot(hid_t[...], work[COT, :, cols(i)]).astype(BF16)
        for k in range(4):
            gdn[i, k] = total[:, 128 * k : 128 * k + 128]

    tiles(n_cols, down_grad)
    if with_dp:
        rs_start(0, 0)
    give_back(TOK, 2, 0)

    def grad_body(i):
        gh = dot(work[COT], wd[ff_tile(i), :], 1, 1)
        gate, up = pre[0, :, ff_tile(i)], pre[1, :, ff_tile(i)]
        s = jax.nn.sigmoid(gate)
        dgu[:, ff_tile(i)] = (gh * up * s * (1.0 + gate * (1.0 - s))).astype(BF16)
        dgu[:, pl.ds(pl.multiple_of(ff + i * 256, 256), 256)] = (gh * (gate * s)).astype(BF16)

    tiles(ff // 256, grad_body)
    give_back(TOK, 2, 1)

    def up_grad(i):
        x = x_t[cols(i), :]
        ggt[i] = dot(x, dgu[:, :ff]).astype(BF16).reshape(4, 128, ff)
        gup[i] = dot(x, dgu[:, ff:]).astype(BF16).reshape(4, 128, ff)

    tiles(n_cols, up_grad)
    if with_dp:
        rs_relay(0, 0)
        rs_start(1, 0, (0, 3))
        rs_start(2, 0, (0, 3))
        rs_start(1, 0, (1, 4))
        rs_start(2, 0, (1, 4))
    give_back(TOK, 1, 0)
    for i in range(n_cols):
        total = dot(dgu[:, :ff], wg[i].reshape(COLS, ff), 1, 1) + dot(dgu[:, ff:], wu[i].reshape(COLS, ff), 1, 1)
        out[COT, :, i * COLS : (i + 1) * COLS] = total.astype(BF16)
        swap_out(COT, i)
    if with_dp:
        rs_finish(0, 0)
        rs_start(0, 1)
    give_back(COT, 4, 0)
    give_back(COT, 4, 1)
    give_back(TOK, 1, 1)
    give_back(COT, 3, 0)
    give_back(COT, 3, 1)
    if with_dp:
        rs_relay(1, 0)
    deliver(TOK, comb_ref, 0)
    deliver(TOK, comb_ref, 1)
    if with_dp:
        rs_relay(2, 0)
    give_back(COT, 2, 0)
    give_back(COT, 2, 1)
    if with_dp:
        rs_relay(0, 1)
    give_back(COT, 1, 0)
    if with_dp:
        rs_finish(1, 0)
        rs_start(1, 1)
    give_back(COT, 1, 1)
    if with_dp:
        rs_finish(0, 1)
        rs_finish(2, 0)
        rs_start(2, 1)
        rs_relay(1, 1)
        rs_relay(2, 1)
        rs_finish(1, 1)
        rs_finish(2, 1)
    else:
        for ref, target in zip(results, (gd_hbm, gg_hbm, gu_hbm)):
            ref[...] = jnp.zeros_like(ref)
            store(ref, target)
    deliver(COT, gtok_ref, 0)
    deliver(COT, gtok_ref, 1)
    for copy in stores:
        copy.wait()
    for copy in sends:
        copy.wait_send()


def hand_over(*refs):
    n = (len(refs) - 1) // 3
    sources, targets, held, sems = refs[:n], refs[n : 2 * n], refs[2 * n : 3 * n], refs[-1]

    def copies(a, b, step):
        every = []
        for i in range(n):
            many = a[i].shape[0] // 2
            for k in range(2):
                piece = pl.ds(k * many, many)
                every.append(pltpu.make_async_copy(a[i].at[piece], b[i].at[piece], sems.at[step, i, k]))
        return every

    loads, stores = copies(sources, held, 0), copies(held, targets, 1)
    for load in loads:
        load.start()
    for load, store in zip(loads, stores):
        load.wait()
        store.start()
    for store in stores:
        store.wait()


def local(tokens, expert_ids, gate_weights, w_gate, w_up, w_down, cotangent):
    rows, width = tokens.shape
    ff = w_gate.shape[2]
    with_dp = lax.axis_size("dp") == 16
    shard = width // 16
    vmem, hbm = pl.BlockSpec(memory_space=pltpu.VMEM), pl.BlockSpec(memory_space=pl.ANY)
    dma = pltpu.SemaphoreType.DMA
    shapes = (
        jax.ShapeDtypeStruct((rows, width), BF16),
        jax.ShapeDtypeStruct((rows, width), BF16),
        jax.ShapeDtypeStruct((shard, ff), F32),
        jax.ShapeDtypeStruct((shard, ff), F32),
        jax.ShapeDtypeStruct((ff, shard), F32),
    )
    outs = pl.pallas_call(
        functools.partial(kernel, with_dp),
        out_shape=shapes,
        in_specs=[vmem] * 4 + [hbm] * 3,
        out_specs=(hbm,) * 5,
        scratch_shapes=[pltpu.VMEM(s.shape, s.dtype) for s in shapes] + [
            pltpu.VMEM((4, 4, shard, ff), BF16),
            pltpu.VMEM((4, 4, shard, ff), BF16),
            pltpu.VMEM((ff, width), BF16),
            pltpu.VMEM((4, 4, ff, shard), BF16),
            pltpu.VMEM((4, 4, shard, ff), BF16),
            pltpu.VMEM((4, 4, shard, ff), BF16),
            pltpu.VMEM((rows, width), BF16),
            pltpu.VMEM((2, 2, HOPS[0], width), BF16),
            pltpu.VMEM((2, 2, ROWS, width), BF16),
            pltpu.VMEM((2, 2, ROWS, width), BF16),
            pltpu.VMEM((2, 5, 8, rows), F32),
            pltpu.VMEM((2, 4, 96, rows), BF16),
            pltpu.VMEM((96, rows), BF16),
            pltpu.VMEM((2, rows, rows), BF16),
            pltpu.VMEM((2, 2 * PAIR, width), BF16),
            pltpu.VMEM((2, PAIR, width), BF16),
            pltpu.VMEM((2, 2 * PAIR, width), BF16),
            pltpu.VMEM((2, PAIR, width), BF16),
            pltpu.VMEM((2, 2 * PAIR, ff), F32),
            pltpu.VMEM((2 * PAIR, ff), BF16),
            pltpu.VMEM((2 * PAIR, 2 * ff), BF16),
            pltpu.VMEM((width, 2 * PAIR), BF16),
            pltpu.VMEM((ff, 2 * PAIR), BF16),
            pltpu.VMEM((2, 2, 6, 2, shard, ff // 2), BF16),
            pltpu.VMEM((2, 2, 6, shard // 2, ff // 2), BF16),
            pltpu.VMEM((2, 6, 2, ff // 2, shard), BF16),
            pltpu.VMEM((2, 6, ff // 4, shard), BF16),
            dma((3,)),
            dma((7,)),
            dma((4, 2, 4, 4)),
            dma((4, 2, 4, 4)),
            dma((2, 4)),
            dma((2, 4)),
            dma((4, 4)),
            dma((4, 4)),
            dma((3, 2, 2, 6)),
            dma((3, 2, 2, 6)),
        ],
        compiler_params=pltpu.CompilerParams(
            collective_id=0, has_side_effects=True, vmem_limit_bytes=63 * 2**20
        ),
    )(
        expert_ids.T, gate_weights.T, tokens, cotangent,
        w_gate.reshape(4, 4, shard, ff), w_up.reshape(4, 4, shard, ff), w_down.reshape(ff, width),
    )
    combined, grad_tokens, grad_gate, grad_up, grad_down = pl.pallas_call(
        hand_over,
        out_shape=shapes,
        in_specs=[hbm] * 5,
        out_specs=(hbm,) * 5,
        scratch_shapes=[pltpu.VMEM(s.shape, s.dtype) for s in shapes] + [dma((2, 5, 2))],
    )(*outs)
    return (combined, grad_tokens, grad_gate[None], grad_up[None], grad_down[None])


def solution(mesh):
    in_specs = (
        P(("dp", "expert"), None),
        P(("dp", "expert"), None),
        P(("dp", "expert"), None),
        P("expert", None, None),
        P("expert", None, None),
        P("expert", None, None),
        P(("dp", "expert"), None),
    )
    out_specs = (
        P(("dp", "expert"), None),
        P(("dp", "expert"), None),
        P("expert", "dp", None),
        P("expert", "dp", None),
        P("expert", None, "dp"),
    )
    return jax.shard_map(local, mesh=mesh, in_specs=in_specs, out_specs=out_specs, check_vma=False)
```

```python
import functools

import jax
import jax.numpy as jnp
from jax import lax
from jax.experimental import pallas as pl
from jax.experimental.pallas import tpu as pltpu
from jax.sharding import PartitionSpec as P

CAP = 24
MESH = pl.DeviceIdType.MESH
F32, BF16 = jnp.float32, jnp.bfloat16
HOPS = (128, 96, 64, 32)
OFFS = (0, HOPS[0], HOPS[0] + HOPS[1], HOPS[0] + HOPS[1] + HOPS[2])
ROWS = sum(HOPS)
PAIR = 8 * CAP
TOK, COT = 0, 1
COLS = 512


def dot(a, b, ca=1, cb=0):
    return lax.dot_general(a, b, (((ca,), (cb,)), ((), ())), preferred_element_type=F32)


def kernel(
    with_dp, idst_ref, gwt_ref, tok_hbm, cot_hbm, wg_hbm, wu_hbm, wd_hbm,
    comb_hbm, gtok_hbm, gg_hbm, gu_hbm, gd_hbm, comb_ref, gtok_ref, gg_ref, gu_ref, gd_ref,
    tok_ref, cot_ref,
    wg, wu, wd, gdn, ggt, gup, scaled, own, ring, back, meta, sel, sel0, place, work, away, out, near, pre, hid, dgu, x_t, hid_t, rs0, rs1, rs0d, rs1d,
    w_sem, o_sem, z_send, z_recv, m_send, m_recv, p_send, p_recv, r_send, r_recv,
):
    rows, width = tok_hbm.shape
    ff = hid.shape[1]
    half = ff // 2
    dp, ex = lax.axis_index("dp"), lax.axis_index("expert")
    core = lax.rem(ex, 2)
    z = lax.div(ex, 2)
    px, py = lax.rem(dp, 4), lax.div(dp, 4)

    def at_z(step):
        return (dp, lax.rem(z + step + 8, 8) * 2 + core)

    partner = (dp, z * 2 + 1 - core)

    def at_dp(axis, step):
        if axis == 0:
            return (py * 4 + lax.rem(px + step + 4, 4), ex)
        return (lax.rem(py + step + 4, 4) * 4 + px, ex)

    load_tok = pltpu.make_async_copy(tok_hbm, tok_ref, w_sem.at[3])
    load_cot = pltpu.make_async_copy(cot_hbm, cot_ref, w_sem.at[4])
    load_tok.start()

    neighbours = [at_z(1), at_z(-1), partner]
    if with_dp:
        neighbours += [at_dp(0, 1), at_dp(0, -1), at_dp(1, 1), at_dp(1, -1)]
    barrier = pltpu.get_barrier_semaphore()
    for device in neighbours:
        pl.semaphore_signal(barrier, inc=1, device_id=device, device_id_type=MESH)
    load_cot.start()
    loads = [
        pltpu.make_async_copy(wg_hbm, wg, w_sem.at[0]),
        pltpu.make_async_copy(wu_hbm, wu, w_sem.at[1]),
        pltpu.make_async_copy(wd_hbm, wd, w_sem.at[2]),
    ]
    for load in loads:
        load.start()

    def distance(e):
        return ((e >> 1) - z) & 7

    i0 = lax.broadcasted_iota(jnp.int32, (rows, rows), 0)
    i1 = lax.broadcasted_iota(jnp.int32, (rows, rows), 1)

    def column(row):
        return jnp.sum(jnp.where(i0 == i1, row, jnp.zeros_like(row)), axis=1, keepdims=True)

    e_r = idst_ref[0:1, :]
    e_c = column(e_r.astype(F32)).astype(jnp.int32)
    weight = column(gwt_ref[0:1, :])
    odd_c, odd_r = e_c & 1, e_r & 1
    d_c, d_r = distance(e_c), distance(e_r)

    def count(lo, hi):
        return jnp.sum(((d_r >= lo) & (d_r <= hi)).astype(F32), axis=1, keepdims=True)

    limit = jnp.minimum(jnp.minimum(HOPS[3], HOPS[2] - count(3, 3)), HOPS[1] - count(2, 3))
    before_c = jnp.sum(((d_r == 4) & (i1 < i0)).astype(F32), axis=1, keepdims=True)
    before_r = jnp.sum(((d_c == 4) & (i0 < i1)).astype(F32), axis=0, keepdims=True)

    def keys(d, before):
        first = before < limit
        plus = jnp.where((d >= 1) & (d <= 3), d, jnp.where((d == 4) & first, 4, 0))
        minus = jnp.where(d >= 5, 8 - d, jnp.where((d == 4) & ~first, 4, 0))
        return plus, minus

    key_c, key_r = keys(d_c, before_c), keys(d_r, before_r)
    same = e_c == e_r
    rank_c = jnp.sum((same & (i1 < i0)).astype(F32), axis=1, keepdims=True)
    rank_r = jnp.sum((same & (i0 < i1)).astype(F32), axis=0, keepdims=True)
    for s in range(2):
        ahead = (key_r[s] > key_c[s]) | ((key_r[s] == key_c[s]) & (i1 < i0))
        pos = jnp.sum(ahead.astype(F32), axis=1, keepdims=True)
        hit = pos == i1.astype(F32)
        place[s] = hit.astype(BF16)
        code = jnp.where(key_c[s] > 0, (64 * key_c[s] + 24 * odd_c).astype(F32) + rank_c, 0.0)
        row = jnp.sum(jnp.where(hit, code, 0.0), axis=0, keepdims=True)
        meta[s, 0] = jnp.broadcast_to(row, meta.shape[2:])

    j = lax.broadcasted_iota(jnp.int32, (96, rows), 0)
    other = j >= 48
    j = jnp.where(other, j - 48, j)
    second = j >= CAP
    j = jnp.where(second, j - CAP, j)
    slot = (j + CAP * jnp.where(other, 1 - core, core)).astype(F32)
    slot_a = jnp.where(second, -9.0, slot)
    slot_b = jnp.where(second, slot, -9.0)
    code0 = jnp.where(d_r == 0, (24 * odd_r).astype(F32) + rank_r, -5.0)
    sel0[...] = (code0 == slot_a).astype(BF16)

    def tiles(n, body):
        def step(i, carry):
            body(i)
            return carry
        lax.fori_loop(0, n, step, 0)

    n_cols = width // COLS

    def cols(i):
        return pl.ds(pl.multiple_of(i * COLS, COLS), COLS)

    def build(kind, i):
        c = slice(i * COLS, (i + 1) * COLS)
        if kind == TOK:
            block = tok_ref[:, c]
        else:
            block = (weight * cot_ref[:, c].astype(F32)).astype(BF16)
            scaled[:, c] = block
        for s in range(2):
            own[kind, s, :, c] = dot(place[s], block, 0, 0).astype(BF16)

    sends = []

    def send(src, dst, ssem, rsem, device, keep=True):
        copy = pltpu.make_async_remote_copy(
            src_ref=src, dst_ref=dst, send_sem=ssem, recv_sem=rsem, device_id=device, device_id_type=MESH
        )
        copy.start()
        if keep:
            sends.append(copy)
        return copy

    metas, moves = {}, {}

    def forward_meta(h):
        for s, step in ((0, 1), (1, -1)):
            metas[s, h] = send(
                meta.at[s, h - 1], meta.at[s, h], m_send.at[s, h - 1], m_recv.at[s, h - 1], at_z(step)
            )

    stores = []

    def store(src, dst):
        copy = pltpu.make_async_copy(src, dst, o_sem.at[len(stores)])
        copy.start()
        stores.append(copy)

    def chunk(q, n):
        return pl.ds(q * (width // n), width // n)

    def forward(kind, h, q=0, n=1):
        many = HOPS[h - 1]
        for s, step in ((0, 1), (1, -1)):
            src = own.at[kind, s] if h == 1 else ring.at[kind, s, pl.ds(OFFS[h - 2], many)]
            dst = ring.at[kind, s, pl.ds(OFFS[h - 1], many)]
            if n > 1:
                src, dst = src.at[:, chunk(q, n)], dst.at[:, chunk(q, n)]
            moves[kind, s, h, q] = send(
                src, dst, z_send.at[kind, s, h - 1, q], z_recv.at[kind, s, h - 1, q], at_z(step), keep=False
            )

    def arrived(kind, h, q=0):
        for s in range(2):
            moves[kind, s, h, q].wait_recv()

    def choose(h):
        for s in range(2):
            metas[s, h].wait_recv()
        for s in range(2):
            slots = slot_b if s == 1 or h == 4 else slot_a
            sel[s, h - 1] = ((meta[s, h, 0:1, :] - 64.0 * h) == slots).astype(BF16)

    def select(kind, h):
        g = h % 4
        lo, n = OFFS[h - 1], HOPS[h - 1]
        source = (tok_ref, scaled)[kind]

        def body(i):
            total = dot(sel[0, h - 1, :, :n], ring[kind, 0, lo : lo + n, cols(i)]) + dot(
                sel[1, h - 1, :, :n], ring[kind, 1, lo : lo + n, cols(i)]
            )
            if h == 4:
                total = total + dot(sel0[...], source[:, cols(i)])
            total = total.astype(BF16)
            work[kind, 48 * g : 48 * g + 48, cols(i)] = total[:48]
            away[kind, 48 * g : 48 * g + 48, cols(i)] = total[48:]

        tiles(n_cols, body)

    pairs = {}

    def swap_in(kind, g):
        pairs[kind, g] = send(
            away.at[kind, pl.ds(48 * g, 48)], work.at[kind, pl.ds(PAIR + 48 * g, 48)],
            p_send.at[kind, g], p_recv.at[kind, g], partner,
        )

    def swap_out(kind, i):
        pairs[2 + kind, i] = send(
            out.at[kind, pl.ds(PAIR, PAIR), chunk(i, 4)], near.at[kind, :, chunk(i, 4)],
            p_send.at[2 + kind, i], p_recv.at[2 + kind, i], partner,
        )

    def swapped(kind):
        for i in range(4):
            pairs[kind, i].wait_recv()

    def group(kind, g, i):
        return jnp.concatenate(
            [out[kind, 48 * g : 48 * g + 48, cols(i)], near[kind, 48 * g : 48 * g + 48, cols(i)]], axis=0
        )

    backs = {}

    def give_back(kind, h, q):
        if h < 4:
            for s in range(2):
                backs[kind, s, h + 1, q].wait_recv()
        else:
            for i in (2 * q, 2 * q + 1):
                pairs[2 + kind, i].wait_recv()
        lo, n = OFFS[h - 1], HOPS[h - 1]

        def body(k):
            i = 2 * q + k
            results = group(kind, h % 4, i)
            for s in range(2):
                total = dot(sel[s, h - 1, :, :n], results, 0, 0)
                if h < 4:
                    far, m = OFFS[h], HOPS[h]
                    ring[kind, s, lo : lo + m, cols(i)] = (
                        total[:m] + back[kind, s, far : far + m, cols(i)].astype(F32)
                    ).astype(BF16)
                    if m < n:
                        ring[kind, s, lo + m : lo + n, cols(i)] = total[m:].astype(BF16)
                else:
                    ring[kind, s, lo : lo + n, cols(i)] = total.astype(BF16)

        tiles(2, body)
        for s, step in ((0, -1), (1, 1)):
            backs[kind, s, h, q] = send(
                ring.at[kind, s, pl.ds(lo, n), chunk(q, 2)], back.at[kind, s, pl.ds(lo, n), chunk(q, 2)],
                z_send.at[2 + kind, s, h - 1, q], z_recv.at[2 + kind, s, h - 1, q], at_z(step),
            )

    def deliver(kind, target, q):
        for s in range(2):
            backs[kind, s, 1, q].wait_recv()

        def body(k):
            i = 2 * q + k
            total = dot(sel0[...], group(kind, 0, i), 0, 0)
            for s in range(2):
                total = total + dot(place[s, :, : HOPS[0]], back[kind, s, : HOPS[0], cols(i)])
            if kind == TOK:
                total = weight * total
            target[:, cols(i)] = total.astype(BF16)

        tiles(2, body)
        store(target.at[:, chunk(q, 2)], (comb_hbm, gtok_hbm)[kind].at[:, chunk(q, 2)])

    grads = (gdn, ggt, gup)
    results = (gd_ref, gg_ref, gu_ref)
    sums = {}

    def place_of(stage, side):
        axis = side if stage == 0 else 1 - side
        return axis, (px, py)[axis]

    def view(m, stage, side, dest, upper):
        c = slice(side * half, (side + 1) * half)
        if m == 0:
            if stage == 0:
                many = slice(2 * upper, 2 * upper + 2)
                return (many, dest, c) if side == 0 else (dest, many, c)
            part = slice(side * half + upper * (half // 2), side * half + (upper + 1) * (half // 2))
            return (dest, px, part) if side == 0 else (py, dest, part)
        if stage == 0:
            many = slice(2 * upper, 2 * upper + 2)
            return (many, dest, slice(None), c) if side == 0 else (dest, many, slice(None), c)
        many = slice(64 * upper, 64 * upper + 64)
        return (dest, px, many, c) if side == 0 else (py, dest, many, c)

    def inbox(m, stage):
        return ((rs0d, rs1d) if m == 0 else (rs0.at[m - 1], rs1.at[m - 1]))[stage]

    def rs_send(m, stage, side, slot):
        axis, p = place_of(stage, side)
        dest, upper, step = (
            (2, 0, 1), (1, 1, 1), (1, 0, 1), (2, 1, -1), (3, 0, -1), (3, 1, -1)
        )[slot]
        where = view(m, stage, side, lax.rem(p + dest, 4), upper)
        sums[m, stage, side, slot] = send(
            grads[m].at[where], inbox(m, stage).at[side, slot],
            r_send.at[m, stage, side, slot], r_recv.at[m, stage, side, slot], at_dp(axis, step),
        )

    def rs_got(m, stage, side, slot):
        sums[m, stage, side, slot].wait_recv()
        return inbox(m, stage)[side, slot].astype(F32)

    def rs_start(m, stage, slots=(0, 3, 1, 4)):
        for slot in slots:
            for side in range(2):
                rs_send(m, stage, side, slot)

    def rs_relay(m, stage):
        for far, dest, upper in ((0, 1, 0), (3, 3, 1)):
            for side in range(2):
                _, p = place_of(stage, side)
                where = view(m, stage, side, lax.rem(p + dest, 4), upper)
                grads[m][where] = (grads[m][where].astype(F32) + rs_got(m, stage, side, far)).astype(BF16)
                rs_send(m, stage, side, far + 2)

    def rs_finish(m, stage):
        for side in range(2):
            _, p = place_of(stage, side)
            totals = []
            for upper, (a, b) in enumerate(((4, 2), (1, 5))):
                where = view(m, stage, side, p, upper)
                total = grads[m][where].astype(F32) + rs_got(m, stage, side, a) + rs_got(m, stage, side, b)
                if stage == 0:
                    grads[m][where] = total.astype(BF16)
                totals.append(total)
            if stage == 1:
                total = jnp.concatenate(totals, axis=0)
                c = slice(side * half, (side + 1) * half)
                if m == 0:
                    gd_ref[c, :] = total
                else:
                    results[m][:, c] = total
        if stage == 1:
            store(results[m], (gd_hbm, gg_hbm, gu_hbm)[m])

    load_tok.wait()
    build(TOK, 0)
    pl.semaphore_wait(barrier, len(neighbours))
    forward_meta(1)
    forward(TOK, 1, 0, 4)
    for i in range(1, 4):
        build(TOK, i)
        forward(TOK, 1, i, 4)
    load_cot.wait()
    for i in range(4):
        build(COT, i)
    forward(COT, 1, 0, 4)
    for h in (1, 2, 3):
        choose(h)
        forward_meta(h + 1)
        for q in range(4 if h == 1 else 1):
            arrived(TOK, h, q)
        forward(TOK, h + 1)
        forward(COT, 1, h, 4)
        if h == 3:
            arrived(COT, 1, 0)
            arrived(COT, 1, 1)
            forward(COT, 2, 0, 2)
        select(TOK, h)
        swap_in(TOK, h)
    choose(4)
    arrived(TOK, 4)
    select(TOK, 4)
    swap_in(TOK, 0)
    for load in loads:
        load.wait()
    arrived(COT, 1, 2)
    arrived(COT, 1, 3)
    forward(COT, 2, 1, 2)
    swapped(TOK)

    def ff_tile(i):
        return pl.ds(pl.multiple_of(i * 256, 256), 256)

    def up_body(i):
        x = work[TOK]
        gate = dot(x, wg[:, :, :, ff_tile(i)].reshape(width, 256))
        up = dot(x, wu[:, :, :, ff_tile(i)].reshape(width, 256))
        pre[0, :, ff_tile(i)] = gate
        pre[1, :, ff_tile(i)] = up
        hid[:, ff_tile(i)] = (gate * jax.nn.sigmoid(gate) * up).astype(BF16)

    tiles(ff // 256, up_body)
    for i in range(n_cols):
        c = slice(i * COLS, (i + 1) * COLS)
        out[TOK, :, c] = dot(hid[...], wd[:, c]).astype(BF16)
        swap_out(TOK, i)
    arrived(COT, 2, 0)
    forward(COT, 3, 0, 2)
    select(COT, 1)
    swap_in(COT, 1)
    arrived(COT, 2, 1)
    forward(COT, 3, 1, 2)

    for s in range(2):
        for h, q in ((1, 0), (1, 1), (1, 2), (1, 3), (2, 0), (3, 0), (4, 0)):
            moves[TOK, s, h, q].wait_send()
    give_back(TOK, 4, 0)
    hid_t[...] = hid[...].T

    def turn(i):
        x_t[cols(i), :] = work[TOK, :, cols(i)].T

    arrived(COT, 3, 0)
    forward(COT, 4, 0, 2)
    select(COT, 2)
    swap_in(COT, 2)
    arrived(COT, 3, 1)
    forward(COT, 4, 1, 2)
    give_back(TOK, 4, 1)
    tiles(n_cols, turn)
    select(COT, 3)
    swap_in(COT, 3)
    give_back(TOK, 3, 0)
    arrived(COT, 4, 0)
    arrived(COT, 4, 1)
    select(COT, 4)
    swap_in(COT, 0)
    for s in range(2):
        for h, q in ((1, 0), (1, 1), (1, 2), (1, 3), (2, 0), (2, 1), (3, 0), (3, 1), (4, 0), (4, 1)):
            moves[COT, s, h, q].wait_send()
    give_back(TOK, 3, 1)
    swapped(COT)

    def down_grad(i):
        total = dot(hid_t[...], work[COT, :, cols(i)]).astype(BF16)
        for k in range(4):
            gdn[i, k] = total[:, 128 * k : 128 * k + 128]

    tiles(n_cols, down_grad)
    if with_dp:
        rs_start(0, 0)
    give_back(TOK, 2, 0)

    def grad_body(i):
        gh = dot(work[COT], wd[ff_tile(i), :], 1, 1)
        gate, up = pre[0, :, ff_tile(i)], pre[1, :, ff_tile(i)]
        s = jax.nn.sigmoid(gate)
        dgu[:, ff_tile(i)] = (gh * up * s * (1.0 + gate * (1.0 - s))).astype(BF16)
        dgu[:, pl.ds(pl.multiple_of(ff + i * 256, 256), 256)] = (gh * (gate * s)).astype(BF16)

    tiles(ff // 256, grad_body)
    give_back(TOK, 2, 1)

    def up_grad(i):
        x = x_t[cols(i), :]
        ggt[i] = dot(x, dgu[:, :ff]).astype(BF16).reshape(4, 128, ff)
        gup[i] = dot(x, dgu[:, ff:]).astype(BF16).reshape(4, 128, ff)

    tiles(n_cols, up_grad)
    if with_dp:
        rs_relay(0, 0)
        rs_start(1, 0, (0, 3))
        rs_start(2, 0, (0, 3))
        rs_start(1, 0, (1, 4))
        rs_start(2, 0, (1, 4))
    give_back(TOK, 1, 0)
    for i in range(n_cols):
        total = dot(dgu[:, :ff], wg[i].reshape(COLS, ff), 1, 1) + dot(dgu[:, ff:], wu[i].reshape(COLS, ff), 1, 1)
        out[COT, :, i * COLS : (i + 1) * COLS] = total.astype(BF16)
        swap_out(COT, i)
    if with_dp:
        rs_finish(0, 0)
        rs_start(0, 1)
    give_back(COT, 4, 0)
    give_back(COT, 4, 1)
    give_back(TOK, 1, 1)
    give_back(COT, 3, 0)
    give_back(COT, 3, 1)
    if with_dp:
        rs_relay(1, 0)
    give_back(COT, 2, 0)
    if with_dp:
        rs_relay(2, 0)
    give_back(COT, 2, 1)
    deliver(TOK, comb_ref, 0)
    deliver(TOK, comb_ref, 1)
    if with_dp:
        rs_relay(0, 1)
        rs_finish(1, 0)
        rs_start(1, 1)
    give_back(COT, 1, 0)
    if with_dp:
        rs_finish(0, 1)
        rs_finish(2, 0)
        rs_start(2, 1)
    give_back(COT, 1, 1)
    if with_dp:
        rs_relay(1, 1)
        rs_relay(2, 1)
        rs_finish(1, 1)
    deliver(COT, gtok_ref, 0)
    if with_dp:
        rs_finish(2, 1)
    else:
        for ref, target in zip(results, (gd_hbm, gg_hbm, gu_hbm)):
            ref[...] = jnp.zeros_like(ref)
            store(ref, target)
    deliver(COT, gtok_ref, 1)
    for copy in stores:
        copy.wait()
    for copy in sends:
        copy.wait_send()


def hand_over(*refs):
    n = (len(refs) - 1) // 3
    sources, targets, held, sems = refs[:n], refs[n : 2 * n], refs[2 * n : 3 * n], refs[-1]

    def copies(a, b, step):
        every = []
        for i in range(n):
            many = a[i].shape[0] // 2
            for k in range(2):
                piece = pl.ds(k * many, many)
                every.append(pltpu.make_async_copy(a[i].at[piece], b[i].at[piece], sems.at[step, i, k]))
        return every

    loads, stores = copies(sources, held, 0), copies(held, targets, 1)
    for load in loads:
        load.start()
    for load, store in zip(loads, stores):
        load.wait()
        store.start()
    for store in stores:
        store.wait()


def local(tokens, expert_ids, gate_weights, w_gate, w_up, w_down, cotangent):
    rows, width = tokens.shape
    ff = w_gate.shape[2]
    with_dp = lax.axis_size("dp") == 16
    shard = width // 16
    vmem, hbm = pl.BlockSpec(memory_space=pltpu.VMEM), pl.BlockSpec(memory_space=pl.ANY)
    dma = pltpu.SemaphoreType.DMA
    shapes = (
        jax.ShapeDtypeStruct((rows, width), BF16),
        jax.ShapeDtypeStruct((rows, width), BF16),
        jax.ShapeDtypeStruct((shard, ff), F32),
        jax.ShapeDtypeStruct((shard, ff), F32),
        jax.ShapeDtypeStruct((ff, shard), F32),
    )
    outs = pl.pallas_call(
        functools.partial(kernel, with_dp),
        out_shape=shapes,
        in_specs=[vmem] * 2 + [hbm] * 5,
        out_specs=(hbm,) * 5,
        scratch_shapes=[pltpu.VMEM(s.shape, s.dtype) for s in shapes] + [
            pltpu.VMEM((rows, width), BF16),
            pltpu.VMEM((rows, width), BF16),
            pltpu.VMEM((4, 4, shard, ff), BF16),
            pltpu.VMEM((4, 4, shard, ff), BF16),
            pltpu.VMEM((ff, width), BF16),
            pltpu.VMEM((4, 4, ff, shard), BF16),
            pltpu.VMEM((4, 4, shard, ff), BF16),
            pltpu.VMEM((4, 4, shard, ff), BF16),
            pltpu.VMEM((rows, width), BF16),
            pltpu.VMEM((2, 2, HOPS[0], width), BF16),
            pltpu.VMEM((2, 2, ROWS, width), BF16),
            pltpu.VMEM((2, 2, ROWS, width), BF16),
            pltpu.VMEM((2, 5, 8, rows), F32),
            pltpu.VMEM((2, 4, 96, rows), BF16),
            pltpu.VMEM((96, rows), BF16),
            pltpu.VMEM((2, rows, rows), BF16),
            pltpu.VMEM((2, 2 * PAIR, width), BF16),
            pltpu.VMEM((2, PAIR, width), BF16),
            pltpu.VMEM((2, 2 * PAIR, width), BF16),
            pltpu.VMEM((2, PAIR, width), BF16),
            pltpu.VMEM((2, 2 * PAIR, ff), F32),
            pltpu.VMEM((2 * PAIR, ff), BF16),
            pltpu.VMEM((2 * PAIR, 2 * ff), BF16),
            pltpu.VMEM((width, 2 * PAIR), BF16),
            pltpu.VMEM((ff, 2 * PAIR), BF16),
            pltpu.VMEM((2, 2, 6, 2, shard, ff // 2), BF16),
            pltpu.VMEM((2, 2, 6, shard // 2, ff // 2), BF16),
            pltpu.VMEM((2, 6, 2, ff // 2, shard), BF16),
            pltpu.VMEM((2, 6, ff // 4, shard), BF16),
            dma((5,)),
            dma((7,)),
            dma((4, 2, 4, 4)),
            dma((4, 2, 4, 4)),
            dma((2, 4)),
            dma((2, 4)),
            dma((4, 4)),
            dma((4, 4)),
            dma((3, 2, 2, 6)),
            dma((3, 2, 2, 6)),
        ],
        compiler_params=pltpu.CompilerParams(
            collective_id=0, has_side_effects=True, vmem_limit_bytes=63 * 2**20
        ),
    )(
        expert_ids.T, gate_weights.T, tokens, cotangent,
        w_gate.reshape(4, 4, shard, ff), w_up.reshape(4, 4, shard, ff), w_down.reshape(ff, width),
    )
    combined, grad_tokens, grad_gate, grad_up, grad_down = pl.pallas_call(
        hand_over,
        out_shape=shapes,
        in_specs=[hbm] * 5,
        out_specs=(hbm,) * 5,
        scratch_shapes=[pltpu.VMEM(s.shape, s.dtype) for s in shapes] + [dma((2, 5, 2))],
    )(*outs)
    return (combined, grad_tokens, grad_gate[None], grad_up[None], grad_down[None])


def solution(mesh):
    in_specs = (
        P(("dp", "expert"), None),
        P(("dp", "expert"), None),
        P(("dp", "expert"), None),
        P("expert", None, None),
        P("expert", None, None),
        P("expert", None, None),
        P(("dp", "expert"), None),
    )
    out_specs = (
        P(("dp", "expert"), None),
        P(("dp", "expert"), None),
        P("expert", "dp", None),
        P("expert", "dp", None),
        P("expert", None, "dp"),
    )
    return jax.shard_map(local, mesh=mesh, in_specs=in_specs, out_specs=out_specs, check_vma=False)
```

```python
import functools

import jax
import jax.numpy as jnp
from jax import lax
from jax.experimental import pallas as pl
from jax.experimental.pallas import tpu as pltpu
from jax.sharding import PartitionSpec as P

CAP = 24
MESH = pl.DeviceIdType.MESH
F32, BF16 = jnp.float32, jnp.bfloat16
HOPS = (128, 96, 64, 32)
OFFS = (0, HOPS[0], HOPS[0] + HOPS[1], HOPS[0] + HOPS[1] + HOPS[2])
ROWS = sum(HOPS)
PAIR = 8 * CAP
TOK, COT = 0, 1
COLS = 512


def dot(a, b, ca=1, cb=0):
    return lax.dot_general(a, b, (((ca,), (cb,)), ((), ())), preferred_element_type=F32)


def kernel(
    with_dp, idst_ref, gwt_ref, tok_hbm, cot_hbm, wg_hbm, wu_hbm, wd_hbm,
    comb_hbm, gtok_hbm, gg_hbm, gu_hbm, gd_hbm, comb_ref, gtok_ref, gg_ref, gu_ref, gd_ref,
    tok_ref, cot_ref,
    wg, wu, wd, gdn, ggt, gup, scaled, own, ring, back, meta, sel, sel0, place, work, away, out, near, pre, hid, dgu, x_t, hid_t, rs0, rs1, rs0d, rs1d,
    w_sem, o_sem, z_send, z_recv, m_send, m_recv, p_send, p_recv, r_send, r_recv,
):
    rows, width = tok_hbm.shape
    ff = hid.shape[1]
    half = ff // 2
    dp, ex = lax.axis_index("dp"), lax.axis_index("expert")
    core = lax.rem(ex, 2)
    z = lax.div(ex, 2)
    px, py = lax.rem(dp, 4), lax.div(dp, 4)

    def at_z(step):
        return (dp, lax.rem(z + step + 8, 8) * 2 + core)

    partner = (dp, z * 2 + 1 - core)

    def at_dp(axis, step):
        if axis == 0:
            return (py * 4 + lax.rem(px + step + 4, 4), ex)
        return (lax.rem(py + step + 4, 4) * 4 + px, ex)

    load_tok = pltpu.make_async_copy(tok_hbm, tok_ref, w_sem.at[3])
    load_cot = pltpu.make_async_copy(cot_hbm, cot_ref, w_sem.at[4])
    load_tok.start()

    neighbours = [at_z(1), at_z(-1), partner]
    if with_dp:
        neighbours += [at_dp(0, 1), at_dp(0, -1), at_dp(1, 1), at_dp(1, -1)]
    barrier = pltpu.get_barrier_semaphore()
    for device in neighbours:
        pl.semaphore_signal(barrier, inc=1, device_id=device, device_id_type=MESH)
    load_cot.start()
    loads = [
        pltpu.make_async_copy(wg_hbm, wg, w_sem.at[0]),
        pltpu.make_async_copy(wu_hbm, wu, w_sem.at[1]),
        pltpu.make_async_copy(wd_hbm, wd, w_sem.at[2]),
    ]
    for load in loads:
        load.start()

    def distance(e):
        return ((e >> 1) - z) & 7

    i0 = lax.broadcasted_iota(jnp.int32, (rows, rows), 0)
    i1 = lax.broadcasted_iota(jnp.int32, (rows, rows), 1)

    def column(row):
        return jnp.sum(jnp.where(i0 == i1, row, jnp.zeros_like(row)), axis=1, keepdims=True)

    e_r = idst_ref[0:1, :]
    e_c = column(e_r.astype(F32)).astype(jnp.int32)
    weight = column(gwt_ref[0:1, :])
    odd_c, odd_r = e_c & 1, e_r & 1
    d_c, d_r = distance(e_c), distance(e_r)

    def count(lo, hi):
        return jnp.sum(((d_r >= lo) & (d_r <= hi)).astype(F32), axis=1, keepdims=True)

    limit = jnp.minimum(jnp.minimum(HOPS[3], HOPS[2] - count(3, 3)), HOPS[1] - count(2, 3))
    before_c = jnp.sum(((d_r == 4) & (i1 < i0)).astype(F32), axis=1, keepdims=True)
    before_r = jnp.sum(((d_c == 4) & (i0 < i1)).astype(F32), axis=0, keepdims=True)

    def keys(d, before):
        first = before < limit
        plus = jnp.where((d >= 1) & (d <= 3), d, jnp.where((d == 4) & first, 4, 0))
        minus = jnp.where(d >= 5, 8 - d, jnp.where((d == 4) & ~first, 4, 0))
        return plus, minus

    key_c, key_r = keys(d_c, before_c), keys(d_r, before_r)
    same = e_c == e_r
    rank_c = jnp.sum((same & (i1 < i0)).astype(F32), axis=1, keepdims=True)
    rank_r = jnp.sum((same & (i0 < i1)).astype(F32), axis=0, keepdims=True)
    for s in range(2):
        ahead = (key_r[s] > key_c[s]) | ((key_r[s] == key_c[s]) & (i1 < i0))
        pos = jnp.sum(ahead.astype(F32), axis=1, keepdims=True)
        hit = pos == i1.astype(F32)
        place[s] = hit.astype(BF16)
        code = jnp.where(key_c[s] > 0, (64 * key_c[s] + 24 * odd_c).astype(F32) + rank_c, 0.0)
        row = jnp.sum(jnp.where(hit, code, 0.0), axis=0, keepdims=True)
        meta[s, 0] = jnp.broadcast_to(row, meta.shape[2:])

    j = lax.broadcasted_iota(jnp.int32, (96, rows), 0)
    other = j >= 48
    j = jnp.where(other, j - 48, j)
    second = j >= CAP
    j = jnp.where(second, j - CAP, j)
    slot = (j + CAP * jnp.where(other, 1 - core, core)).astype(F32)
    slot_a = jnp.where(second, -9.0, slot)
    slot_b = jnp.where(second, slot, -9.0)
    code0 = jnp.where(d_r == 0, (24 * odd_r).astype(F32) + rank_r, -5.0)
    sel0[...] = (code0 == slot_a).astype(BF16)

    def tiles(n, body):
        def step(i, carry):
            body(i)
            return carry
        lax.fori_loop(0, n, step, 0)

    n_cols = width // COLS

    def cols(i):
        return pl.ds(pl.multiple_of(i * COLS, COLS), COLS)

    def build(kind, i):
        c = slice(i * COLS, (i + 1) * COLS)
        if kind == TOK:
            block = tok_ref[:, c]
        else:
            block = (weight * cot_ref[:, c].astype(F32)).astype(BF16)
            scaled[:, c] = block
        for s in range(2):
            own[kind, s, :, c] = dot(place[s], block, 0, 0).astype(BF16)

    sends = []

    def send(src, dst, ssem, rsem, device, keep=True):
        copy = pltpu.make_async_remote_copy(
            src_ref=src, dst_ref=dst, send_sem=ssem, recv_sem=rsem, device_id=device, device_id_type=MESH
        )
        copy.start()
        if keep:
            sends.append(copy)
        return copy

    metas, moves = {}, {}

    def forward_meta(h):
        for s, step in ((0, 1), (1, -1)):
            metas[s, h] = send(
                meta.at[s, h - 1], meta.at[s, h], m_send.at[s, h - 1], m_recv.at[s, h - 1], at_z(step)
            )

    stores = []

    def store(src, dst):
        copy = pltpu.make_async_copy(src, dst, o_sem.at[len(stores)])
        copy.start()
        stores.append(copy)

    def chunk(q, n):
        return pl.ds(q * (width // n), width // n)

    def forward(kind, h, q=0, n=1):
        many = HOPS[h - 1]
        for s, step in ((0, 1), (1, -1)):
            src = own.at[kind, s] if h == 1 else ring.at[kind, s, pl.ds(OFFS[h - 2], many)]
            dst = ring.at[kind, s, pl.ds(OFFS[h - 1], many)]
            if n > 1:
                src, dst = src.at[:, chunk(q, n)], dst.at[:, chunk(q, n)]
            moves[kind, s, h, q] = send(
                src, dst, z_send.at[kind, s, h - 1, q], z_recv.at[kind, s, h - 1, q], at_z(step), keep=False
            )

    def arrived(kind, h, q=0):
        for s in range(2):
            moves[kind, s, h, q].wait_recv()

    def choose(h):
        for s in range(2):
            metas[s, h].wait_recv()
        for s in range(2):
            slots = slot_b if s == 1 or h == 4 else slot_a
            sel[s, h - 1] = ((meta[s, h, 0:1, :] - 64.0 * h) == slots).astype(BF16)

    def select(kind, h):
        g = h % 4
        lo, n = OFFS[h - 1], HOPS[h - 1]
        source = (tok_ref, scaled)[kind]

        def body(i):
            total = dot(sel[0, h - 1, :, :n], ring[kind, 0, lo : lo + n, cols(i)]) + dot(
                sel[1, h - 1, :, :n], ring[kind, 1, lo : lo + n, cols(i)]
            )
            if h == 4:
                total = total + dot(sel0[...], source[:, cols(i)])
            total = total.astype(BF16)
            work[kind, 48 * g : 48 * g + 48, cols(i)] = total[:48]
            away[kind, 48 * g : 48 * g + 48, cols(i)] = total[48:]

        tiles(n_cols, body)

    pairs = {}

    def swap_in(kind, g):
        pairs[kind, g] = send(
            away.at[kind, pl.ds(48 * g, 48)], work.at[kind, pl.ds(PAIR + 48 * g, 48)],
            p_send.at[kind, g], p_recv.at[kind, g], partner,
        )

    def swap_out(kind, i):
        pairs[2 + kind, i] = send(
            out.at[kind, pl.ds(PAIR, PAIR), chunk(i, 4)], near.at[kind, :, chunk(i, 4)],
            p_send.at[2 + kind, i], p_recv.at[2 + kind, i], partner,
        )

    def swapped(kind):
        for i in range(4):
            pairs[kind, i].wait_recv()

    def group(kind, g, i):
        return jnp.concatenate(
            [out[kind, 48 * g : 48 * g + 48, cols(i)], near[kind, 48 * g : 48 * g + 48, cols(i)]], axis=0
        )

    backs = {}

    def give_back(kind, h, q):
        if h < 4:
            for s in range(2):
                backs[kind, s, h + 1, q].wait_recv()
        else:
            for i in (2 * q, 2 * q + 1):
                pairs[2 + kind, i].wait_recv()
        lo, n = OFFS[h - 1], HOPS[h - 1]

        def body(k):
            i = 2 * q + k
            results = group(kind, h % 4, i)
            for s in range(2):
                total = dot(sel[s, h - 1, :, :n], results, 0, 0)
                if h < 4:
                    far, m = OFFS[h], HOPS[h]
                    ring[kind, s, lo : lo + m, cols(i)] = (
                        total[:m] + back[kind, s, far : far + m, cols(i)].astype(F32)
                    ).astype(BF16)
                    if m < n:
                        ring[kind, s, lo + m : lo + n, cols(i)] = total[m:].astype(BF16)
                else:
                    ring[kind, s, lo : lo + n, cols(i)] = total.astype(BF16)

        tiles(2, body)
        for s, step in ((0, -1), (1, 1)):
            backs[kind, s, h, q] = send(
                ring.at[kind, s, pl.ds(lo, n), chunk(q, 2)], back.at[kind, s, pl.ds(lo, n), chunk(q, 2)],
                z_send.at[2 + kind, s, h - 1, q], z_recv.at[2 + kind, s, h - 1, q], at_z(step),
            )

    def deliver(kind, target, q):
        for s in range(2):
            backs[kind, s, 1, q].wait_recv()

        def body(k):
            i = 2 * q + k
            total = dot(sel0[...], group(kind, 0, i), 0, 0)
            for s in range(2):
                total = total + dot(place[s, :, : HOPS[0]], back[kind, s, : HOPS[0], cols(i)])
            if kind == TOK:
                total = weight * total
            target[:, cols(i)] = total.astype(BF16)

        tiles(2, body)
        store(target.at[:, chunk(q, 2)], (comb_hbm, gtok_hbm)[kind].at[:, chunk(q, 2)])

    grads = (gdn, ggt, gup)
    results = (gd_ref, gg_ref, gu_ref)
    sums = {}

    def place_of(stage, side):
        axis = side if stage == 0 else 1 - side
        return axis, (px, py)[axis]

    def view(m, stage, side, dest, upper):
        c = slice(side * half, (side + 1) * half)
        if m == 0:
            if stage == 0:
                many = slice(2 * upper, 2 * upper + 2)
                return (many, dest, c) if side == 0 else (dest, many, c)
            part = slice(side * half + upper * (half // 2), side * half + (upper + 1) * (half // 2))
            return (dest, px, part) if side == 0 else (py, dest, part)
        if stage == 0:
            many = slice(2 * upper, 2 * upper + 2)
            return (many, dest, slice(None), c) if side == 0 else (dest, many, slice(None), c)
        many = slice(64 * upper, 64 * upper + 64)
        return (dest, px, many, c) if side == 0 else (py, dest, many, c)

    def inbox(m, stage):
        return ((rs0d, rs1d) if m == 0 else (rs0.at[m - 1], rs1.at[m - 1]))[stage]

    def rs_send(m, stage, side, slot):
        axis, p = place_of(stage, side)
        dest, upper, step = (
            (2, 0, 1), (1, 1, 1), (1, 0, 1), (2, 1, -1), (3, 0, -1), (3, 1, -1)
        )[slot]
        where = view(m, stage, side, lax.rem(p + dest, 4), upper)
        sums[m, stage, side, slot] = send(
            grads[m].at[where], inbox(m, stage).at[side, slot],
            r_send.at[m, stage, side, slot], r_recv.at[m, stage, side, slot], at_dp(axis, step),
        )

    def rs_got(m, stage, side, slot):
        sums[m, stage, side, slot].wait_recv()
        return inbox(m, stage)[side, slot].astype(F32)

    def rs_start(m, stage, slots=(0, 3, 1, 4)):
        for slot in slots:
            for side in range(2):
                rs_send(m, stage, side, slot)

    def rs_relay(m, stage):
        for far, dest, upper in ((0, 1, 0), (3, 3, 1)):
            for side in range(2):
                _, p = place_of(stage, side)
                where = view(m, stage, side, lax.rem(p + dest, 4), upper)
                grads[m][where] = (grads[m][where].astype(F32) + rs_got(m, stage, side, far)).astype(BF16)
                rs_send(m, stage, side, far + 2)

    def rs_finish(m, stage):
        for side in range(2):
            _, p = place_of(stage, side)
            totals = []
            for upper, (a, b) in enumerate(((4, 2), (1, 5))):
                where = view(m, stage, side, p, upper)
                total = grads[m][where].astype(F32) + rs_got(m, stage, side, a) + rs_got(m, stage, side, b)
                if stage == 0:
                    grads[m][where] = total.astype(BF16)
                totals.append(total)
            if stage == 1:
                total = jnp.concatenate(totals, axis=0)
                c = slice(side * half, (side + 1) * half)
                if m == 0:
                    gd_ref[c, :] = total
                else:
                    results[m][:, c] = total
        if stage == 1:
            store(results[m], (gd_hbm, gg_hbm, gu_hbm)[m])

    load_tok.wait()
    build(TOK, 0)
    pl.semaphore_wait(barrier, len(neighbours))
    forward_meta(1)
    forward(TOK, 1, 0, 4)
    for i in range(1, 4):
        build(TOK, i)
        forward(TOK, 1, i, 4)
    load_cot.wait()
    for i in range(4):
        build(COT, i)
    forward(COT, 1, 0, 4)
    for h in (1, 2, 3):
        choose(h)
        forward_meta(h + 1)
        for q in range(4 if h == 1 else 1):
            arrived(TOK, h, q)
        forward(TOK, h + 1)
        forward(COT, 1, h, 4)
        if h == 3:
            arrived(COT, 1, 0)
            arrived(COT, 1, 1)
            forward(COT, 2, 0, 2)
        select(TOK, h)
        swap_in(TOK, h)
    choose(4)
    arrived(TOK, 4)
    select(TOK, 4)
    swap_in(TOK, 0)
    for load in loads:
        load.wait()
    arrived(COT, 1, 2)
    arrived(COT, 1, 3)
    forward(COT, 2, 1, 2)
    swapped(TOK)

    def ff_tile(i):
        return pl.ds(pl.multiple_of(i * 256, 256), 256)

    def up_body(i):
        x = work[TOK]
        gate = dot(x, wg[:, :, :, ff_tile(i)].reshape(width, 256))
        up = dot(x, wu[:, :, :, ff_tile(i)].reshape(width, 256))
        pre[0, :, ff_tile(i)] = gate
        pre[1, :, ff_tile(i)] = up
        hid[:, ff_tile(i)] = (gate * jax.nn.sigmoid(gate) * up).astype(BF16)

    tiles(ff // 256, up_body)
    for i in range(n_cols):
        c = slice(i * COLS, (i + 1) * COLS)
        out[TOK, :, c] = dot(hid[...], wd[:, c]).astype(BF16)
        swap_out(TOK, i)
    arrived(COT, 2, 0)
    forward(COT, 3, 0, 2)
    select(COT, 1)
    swap_in(COT, 1)
    arrived(COT, 2, 1)
    forward(COT, 3, 1, 2)

    for s in range(2):
        for h, q in ((1, 0), (1, 1), (1, 2), (1, 3), (2, 0), (3, 0), (4, 0)):
            moves[TOK, s, h, q].wait_send()
    give_back(TOK, 4, 0)
    hid_t[...] = hid[...].T

    def turn(i):
        x_t[cols(i), :] = work[TOK, :, cols(i)].T

    arrived(COT, 3, 0)
    forward(COT, 4, 0, 2)
    select(COT, 2)
    swap_in(COT, 2)
    arrived(COT, 3, 1)
    forward(COT, 4, 1, 2)
    give_back(TOK, 4, 1)
    tiles(n_cols, turn)
    select(COT, 3)
    swap_in(COT, 3)
    give_back(TOK, 3, 0)
    arrived(COT, 4, 0)
    arrived(COT, 4, 1)
    select(COT, 4)
    swap_in(COT, 0)
    for s in range(2):
        for h, q in ((1, 0), (1, 1), (1, 2), (1, 3), (2, 0), (2, 1), (3, 0), (3, 1), (4, 0), (4, 1)):
            moves[COT, s, h, q].wait_send()
    give_back(TOK, 3, 1)
    swapped(COT)

    def down_grad(i):
        total = dot(hid_t[...], work[COT, :, cols(i)]).astype(BF16)
        for k in range(4):
            gdn[i, k] = total[:, 128 * k : 128 * k + 128]

    tiles(n_cols, down_grad)
    if with_dp:
        rs_start(0, 0)
    give_back(TOK, 2, 0)

    def grad_body(i):
        gh = dot(work[COT], wd[ff_tile(i), :], 1, 1)
        gate, up = pre[0, :, ff_tile(i)], pre[1, :, ff_tile(i)]
        s = jax.nn.sigmoid(gate)
        dgu[:, ff_tile(i)] = (gh * up * s * (1.0 + gate * (1.0 - s))).astype(BF16)
        dgu[:, pl.ds(pl.multiple_of(ff + i * 256, 256), 256)] = (gh * (gate * s)).astype(BF16)

    tiles(ff // 256, grad_body)
    give_back(TOK, 2, 1)

    def up_grad(i):
        x = x_t[cols(i), :]
        ggt[i] = dot(x, dgu[:, :ff]).astype(BF16).reshape(4, 128, ff)
        gup[i] = dot(x, dgu[:, ff:]).astype(BF16).reshape(4, 128, ff)

    tiles(n_cols, up_grad)
    if with_dp:
        rs_relay(0, 0)
        rs_start(1, 0, (0, 3))
        rs_start(2, 0, (0, 3))
        rs_start(1, 0, (1, 4))
        rs_start(2, 0, (1, 4))
    give_back(TOK, 1, 0)
    for i in range(n_cols):
        total = dot(dgu[:, :ff], wg[i].reshape(COLS, ff), 1, 1) + dot(dgu[:, ff:], wu[i].reshape(COLS, ff), 1, 1)
        out[COT, :, i * COLS : (i + 1) * COLS] = total.astype(BF16)
        swap_out(COT, i)
    if with_dp:
        rs_finish(0, 0)
        rs_start(0, 1)
    give_back(COT, 4, 0)
    give_back(COT, 4, 1)
    give_back(TOK, 1, 1)
    give_back(COT, 3, 0)
    give_back(COT, 3, 1)
    if with_dp:
        rs_relay(1, 0)
    give_back(COT, 2, 0)
    if with_dp:
        rs_relay(2, 0)
    give_back(COT, 2, 1)
    deliver(TOK, comb_ref, 0)
    deliver(TOK, comb_ref, 1)
    if with_dp:
        rs_relay(0, 1)
        rs_finish(1, 0)
        rs_start(1, 1)
    give_back(COT, 1, 0)
    if with_dp:
        rs_finish(0, 1)
        rs_finish(2, 0)
        rs_start(2, 1)
    give_back(COT, 1, 1)
    if with_dp:
        rs_relay(1, 1)
        rs_relay(2, 1)
        rs_finish(1, 1)
    deliver(COT, gtok_ref, 0)
    if with_dp:
        rs_finish(2, 1)
    else:
        for ref, target in zip(results, (gd_hbm, gg_hbm, gu_hbm)):
            ref[...] = jnp.zeros_like(ref)
            store(ref, target)
    deliver(COT, gtok_ref, 1)
    for copy in stores:
        copy.wait()
    for copy in sends:
        copy.wait_send()


def hand_over(*refs):
    n = (len(refs) - 1) // 3
    sources, targets, held, sems = refs[:n], refs[n : 2 * n], refs[2 * n : 3 * n], refs[-1]

    def copies(a, b, step):
        every = []
        for i in range(n):
            many = a[i].shape[0] // 4
            for k in range(4):
                piece = pl.ds(k * many, many)
                every.append(pltpu.make_async_copy(a[i].at[piece], b[i].at[piece], sems.at[step, i, k]))
        return every

    loads, stores = copies(sources, held, 0), copies(held, targets, 1)
    for load in loads:
        load.start()
    for load, store in zip(loads, stores):
        load.wait()
        store.start()
    for store in stores:
        store.wait()


def local(tokens, expert_ids, gate_weights, w_gate, w_up, w_down, cotangent):
    rows, width = tokens.shape
    ff = w_gate.shape[2]
    with_dp = lax.axis_size("dp") == 16
    shard = width // 16
    vmem, hbm = pl.BlockSpec(memory_space=pltpu.VMEM), pl.BlockSpec(memory_space=pl.ANY)
    dma = pltpu.SemaphoreType.DMA
    shapes = (
        jax.ShapeDtypeStruct((rows, width), BF16),
        jax.ShapeDtypeStruct((rows, width), BF16),
        jax.ShapeDtypeStruct((shard, ff), F32),
        jax.ShapeDtypeStruct((shard, ff), F32),
        jax.ShapeDtypeStruct((ff, shard), F32),
    )
    outs = pl.pallas_call(
        functools.partial(kernel, with_dp),
        out_shape=shapes,
        in_specs=[vmem] * 2 + [hbm] * 5,
        out_specs=(hbm,) * 5,
        scratch_shapes=[pltpu.VMEM(s.shape, s.dtype) for s in shapes] + [
            pltpu.VMEM((rows, width), BF16),
            pltpu.VMEM((rows, width), BF16),
            pltpu.VMEM((4, 4, shard, ff), BF16),
            pltpu.VMEM((4, 4, shard, ff), BF16),
            pltpu.VMEM((ff, width), BF16),
            pltpu.VMEM((4, 4, ff, shard), BF16),
            pltpu.VMEM((4, 4, shard, ff), BF16),
            pltpu.VMEM((4, 4, shard, ff), BF16),
            pltpu.VMEM((rows, width), BF16),
            pltpu.VMEM((2, 2, HOPS[0], width), BF16),
            pltpu.VMEM((2, 2, ROWS, width), BF16),
            pltpu.VMEM((2, 2, ROWS, width), BF16),
            pltpu.VMEM((2, 5, 8, rows), F32),
            pltpu.VMEM((2, 4, 96, rows), BF16),
            pltpu.VMEM((96, rows), BF16),
            pltpu.VMEM((2, rows, rows), BF16),
            pltpu.VMEM((2, 2 * PAIR, width), BF16),
            pltpu.VMEM((2, PAIR, width), BF16),
            pltpu.VMEM((2, 2 * PAIR, width), BF16),
            pltpu.VMEM((2, PAIR, width), BF16),
            pltpu.VMEM((2, 2 * PAIR, ff), F32),
            pltpu.VMEM((2 * PAIR, ff), BF16),
            pltpu.VMEM((2 * PAIR, 2 * ff), BF16),
            pltpu.VMEM((width, 2 * PAIR), BF16),
            pltpu.VMEM((ff, 2 * PAIR), BF16),
            pltpu.VMEM((2, 2, 6, 2, shard, ff // 2), BF16),
            pltpu.VMEM((2, 2, 6, shard // 2, ff // 2), BF16),
            pltpu.VMEM((2, 6, 2, ff // 2, shard), BF16),
            pltpu.VMEM((2, 6, ff // 4, shard), BF16),
            dma((5,)),
            dma((7,)),
            dma((4, 2, 4, 4)),
            dma((4, 2, 4, 4)),
            dma((2, 4)),
            dma((2, 4)),
            dma((4, 4)),
            dma((4, 4)),
            dma((3, 2, 2, 6)),
            dma((3, 2, 2, 6)),
        ],
        compiler_params=pltpu.CompilerParams(
            collective_id=0, has_side_effects=True, vmem_limit_bytes=63 * 2**20
        ),
    )(
        expert_ids.T, gate_weights.T, tokens, cotangent,
        w_gate.reshape(4, 4, shard, ff), w_up.reshape(4, 4, shard, ff), w_down.reshape(ff, width),
    )
    combined, grad_tokens, grad_gate, grad_up, grad_down = pl.pallas_call(
        hand_over,
        out_shape=shapes,
        in_specs=[hbm] * 5,
        out_specs=(hbm,) * 5,
        scratch_shapes=[pltpu.VMEM(s.shape, s.dtype) for s in shapes] + [dma((2, 5, 4))],
    )(*outs)
    return (combined, grad_tokens, grad_gate[None], grad_up[None], grad_down[None])


def solution(mesh):
    in_specs = (
        P(("dp", "expert"), None),
        P(("dp", "expert"), None),
        P(("dp", "expert"), None),
        P("expert", None, None),
        P("expert", None, None),
        P("expert", None, None),
        P(("dp", "expert"), None),
    )
    out_specs = (
        P(("dp", "expert"), None),
        P(("dp", "expert"), None),
        P("expert", "dp", None),
        P("expert", "dp", None),
        P("expert", None, "dp"),
    )
    return jax.shard_map(local, mesh=mesh, in_specs=in_specs, out_specs=out_specs, check_vma=False)
```
